1024 devices in a mesh: dp: 16 (over y, x_hi), exp: 2 (over core), etp: 32 (over z, x_lo).
Axes of the slice: x: 8 (x_hi: 2, x_lo: 4; x = x_hi * 4 + x_lo), y: 8, z: 8, core: 2. Of those that a mesh axis runs over, the one named last changes fastest.
Arguments:
- tokens: bfloat16 [4096, 4096], P('etp', 'dp'), may hold values from -6 to 6
- routes: int32 [4096, 2], P('etp'), may hold values from 0 to 63, all different within a row; in each aligned block of 128 rows (0 to 127, 128 to 255, ...) at most 8 rows name the same one
- route_weights: float32 [4096, 2], P('etp'), may hold values from 0.2 to 1
- gate_weight: bfloat16 [64, 4096, 1536], P('etp', 'dp', 'exp'), may hold values from -0.09375 to 0.09375
- up_weight: bfloat16 [64, 4096, 1536], P('etp', 'dp', 'exp'), may hold values from -0.09375 to 0.09375
- down_weight: bfloat16 [64, 1536, 4096], P('etp', 'exp', 'dp'), may hold values from -0.15625 to 0.15625
- cotangent: bfloat16 [4096, 4096], P('etp', 'dp'), may hold values from -6 to 6
Outputs:
- mixed: bfloat16 [4096, 4096], P('etp', ('dp', 'exp'))
- d_tokens: bfloat16 [4096, 4096], P('etp', ('dp', 'exp'))
- d_down: bfloat16 [64, 1536, 4096], P('etp', 'exp', 'dp')
The draws below stay inside these ranges and needn't reach their ends.
Inputs may be any that keep to these rules, and one draw needn't show every extreme that they name: `routes`: each row names 2 different experts. Within the rows of one group of 128 consecutive tokens no expert is named by more than 8 rows; in every draw some group names some expert exactly 8 times.
All inputs are finite; a program needn't handle non-finite values.
Results may differ from the reference program's by a relative error of at most 0.012.
Values may be sent and summed in bfloat16 or wider, within the bound.
No kernel may reach another device: no remote copies, remote signals or barrier semaphores. Data moves between devices by JAX's collectives and lax.ppermute only.
A program may use at most 32 MiB of HBM per device.

```python
import math
import jax
import jax.numpy as jnp
import numpy as np
from jax import lax

D = 4096
FF = 1536
TOP = 2
TOK_GRP = 128
EXPERTS = 64
CAP = 8
FF_DEV = 768
TOKENS = 4096
N_EXP = 2
N_ETP = 32


def levels(stream_key, dims, shards, low, largest):
    gain, own = 1.0, jax.random.fold_in(stream_key, 6)
    for dim, blocks in shards:
        heights = jnp.exp(jax.random.uniform(jax.random.fold_in(own, dim), (blocks,), jnp.float32, low / len(shards), largest / len(shards)))
        gain = gain * jnp.repeat(heights, dims[dim] // blocks).reshape([-1 if axis == dim else 1 for axis in range(len(dims))])
    return gain


def deal_out(rng, own, number, rows, number_of, top, reach, skew):
    order = jax.random.permutation(rng, number_of)
    crowded, usual = load_shares(number_of, rows * top, reach, skew, True), load_shares(number_of, rows * top, reach, skew, False)
    places = jnp.arange(number_of)

    def named(tallies, offset_by):
        used = int((tallies > 0).sum())
        fixed = max(1, used // 4)
        passed = fixed + (places - fixed + offset_by * (used - fixed)) % max(1, number_of - fixed)
        return jnp.zeros((number_of,), jnp.int32).at[order[jnp.where(places < fixed, places, passed)]].set(jnp.asarray(tallies, jnp.int32))

    tallies = jnp.where(number % 4 == 0, named(crowded, number // 4), named(usual, number - number // 4 - 1))
    mixed = jax.random.permutation(jax.random.fold_in(own, 3), number_of)
    source_of, receiver = mixed[0:number_of // 2 * 2:2], mixed[1:number_of // 2 * 2:2]
    room = jnp.minimum(tallies[source_of] - 1, reach - tallies[receiver]) // 2
    room = jnp.where((source_of == order[0]) | (receiver == order[0]) | (tallies[receiver] == 0), 0, jnp.maximum(room, 0))
    passed = jax.random.randint(jax.random.fold_in(own, 4), (number_of // 2,), 0, 1 << 20) % (room + 1)
    tallies = tallies.at[source_of].add(-passed).at[receiver].add(passed)
    labels = jnp.searchsorted(jnp.cumsum(tallies), jnp.arange(rows * top), side="right").astype(jnp.int32)
    table = labels.reshape(top, rows).T
    table = table[jax.random.permutation(jax.random.fold_in(own, 1), rows)]
    offset_by = jax.random.randint(jax.random.fold_in(own, 2), (rows, 1), 0, top)
    return jnp.take_along_axis(table, (jnp.arange(top)[None, :] + offset_by) % top, axis=1)


def load_shares(number_of, total, limit, slope, full):
    portions = [(1 << 20) // math.isqrt(rank ** slope) + 1 for rank in range(1, number_of + 1)]
    largest = limit if full else min(limit, max(-(-total // number_of), total * portions[0] // sum(portions)))
    least = 1 if total - largest >= number_of - 1 else 0
    holding, surplus = [largest] + [least] * (number_of - 1), total - largest - least * (number_of - 1)
    while surplus > 0:
        free = [i for i in range(1, number_of) if holding[i] < largest] or [i for i in range(1, number_of) if holding[i] < limit]
        pool, budget = sum([portions[i] for i in free]), surplus
        for i in free:
            addition = min(limit - holding[i], max(1, budget * portions[i] // pool), surplus)
            holding[i] = holding[i] + addition
            surplus = surplus - addition
    return np.array(holding)


def gaussian(stream_key, dims, deviation, bound, cuts=(), kind=jnp.bfloat16):
    array = jax.random.normal(stream_key, dims, jnp.float32) * deviation
    if len(cuts) > 0:
        array = levels(stream_key, dims, cuts, -0.22, 0.18) * array
    return jnp.clip(array, min=-bound, max=bound).astype(kind)


def setup_inputs(seed: int = 0) -> dict:
    key_of = jax.random.split(jax.random.key(seed), 8)
    tokens = gaussian(key_of[0], (TOKENS, D), 1.0, 6.0, ((0, 32), (1, 16)))
    routes_keys = jax.random.split(jax.random.fold_in(key_of[1], 1), TOKENS // TOK_GRP)
    routes_turns = jax.random.permutation(jax.random.fold_in(key_of[1], 3), TOKENS // TOK_GRP)
    routes = jax.vmap(lambda own, number: deal_out(jax.random.fold_in(key_of[1], 2), own, number, TOK_GRP, EXPERTS, TOP, CAP, 2))(routes_keys, routes_turns).reshape((TOKENS, TOP))
    route_weights = jnp.clip(0.2 + 0.8 * jax.random.uniform(key_of[2], (TOKENS, TOP), jnp.float32) ** levels(key_of[2], (TOKENS, TOP), ((0, 32),), -0.2, 0.2), 0.2, 1.0)
    gate_weight = gaussian(key_of[3], (EXPERTS, D, FF), D ** -0.5, 0.09375, ((0, 32), (1, 16), (2, 2)))
    up_weight = gaussian(key_of[4], (EXPERTS, D, FF), D ** -0.5, 0.09375, ((0, 32), (1, 16), (2, 2)))
    down_weight = gaussian(key_of[5], (EXPERTS, FF, D), FF ** -0.5, 0.15625, ((0, 32), (1, 2), (2, 16)))
    cotangent = gaussian(key_of[6], (TOKENS, D), 1.0, 6.0, ((0, 32), (1, 16)))
    return dict(tokens=tokens, routes=routes, route_weights=route_weights, gate_weight=gate_weight, up_weight=up_weight, down_weight=down_weight, cotangent=cotangent)


def rounded(values):
    return lax.optimization_barrier(values.astype(jnp.bfloat16)).astype(jnp.float32)


def expert_pass(inputs):
    rows_in, rows_grad, w_gate, w_up, w_down = inputs
    gate = jnp.dot(rows_in, w_gate, preferred_element_type=jnp.float32)
    up_proj = jnp.dot(rows_in, w_up, preferred_element_type=jnp.float32)
    sigmoid_gate = jax.nn.sigmoid(gate)
    silu_gate = gate * sigmoid_gate
    hidden = (silu_gate * up_proj).astype(jnp.bfloat16)
    row_count = hidden.shape[0]
    hidden_blocks = hidden.reshape(row_count, N_EXP, FF_DEV).astype(jnp.float32)
    down_blocks = w_down.reshape(N_EXP, FF_DEV, D).astype(jnp.float32)
    out_part = jnp.einsum('rbf,bfd->brd', hidden_blocks, down_blocks, precision=lax.Precision.HIGHEST)
    slot_out = jnp.sum(rounded(out_part), axis=0)
    d_hidden = jnp.dot(rows_grad, w_down.T, preferred_element_type=jnp.float32)
    d_up = (d_hidden * silu_gate).astype(jnp.bfloat16)
    d_gate = (d_hidden * up_proj * sigmoid_gate * (1.0 + gate * (1.0 - sigmoid_gate))).astype(jnp.bfloat16)
    gate_blocks = w_gate.reshape(D, N_EXP, FF_DEV).astype(jnp.float32)
    up_blocks = w_up.reshape(D, N_EXP, FF_DEV).astype(jnp.float32)
    grad_part = jnp.einsum('rbf,dbf->brd', d_gate.reshape(row_count, N_EXP, FF_DEV).astype(jnp.float32), gate_blocks, precision=lax.Precision.HIGHEST)
    grad_part = grad_part + jnp.einsum('rbf,dbf->brd', d_up.reshape(row_count, N_EXP, FF_DEV).astype(jnp.float32), up_blocks, precision=lax.Precision.HIGHEST)
    slot_back = jnp.sum(rounded(grad_part), axis=0)
    d_down = jnp.dot(hidden.T, rows_grad, preferred_element_type=jnp.float32).astype(jnp.bfloat16)
    return slot_out, slot_back, d_down


def reference(tokens, routes, route_weights, gate_weight, up_weight, down_weight, cotangent):
    groups = N_ETP
    pairs = TOK_GRP * TOP
    slots_all = EXPERTS * CAP
    routes_grp = routes.reshape(groups, pairs)
    expert_hot = (routes_grp[:, :, None] == jnp.arange(EXPERTS, dtype=jnp.int32)[None, None, :]).astype(jnp.int32)
    position = jnp.sum((jnp.cumsum(expert_hot, axis=1) - 1) * expert_hot, axis=2)
    slot_index = (routes_grp * CAP + position).astype(jnp.int32)
    token_rows = jnp.repeat(tokens.reshape(groups, TOK_GRP, D), TOP, axis=1)
    grad_rows = (route_weights.reshape(groups, pairs, 1) * jnp.repeat(cotangent.reshape(groups, TOK_GRP, D).astype(jnp.float32), TOP, axis=1)).astype(jnp.bfloat16)
    group_ids = jnp.arange(groups, dtype=jnp.int32)[:, None]
    slot_tokens = jnp.zeros((groups, slots_all, D), jnp.bfloat16).at[group_ids, slot_index].set(token_rows)
    slot_grads = jnp.zeros((groups, slots_all, D), jnp.bfloat16).at[group_ids, slot_index].set(grad_rows)
    expert_in = slot_tokens.reshape(groups, EXPERTS, CAP, D).transpose(1, 0, 2, 3).reshape(EXPERTS, groups * CAP, D)
    expert_grad = slot_grads.reshape(groups, EXPERTS, CAP, D).transpose(1, 0, 2, 3).reshape(EXPERTS, groups * CAP, D)
    slot_out, slot_back, d_down = lax.map(expert_pass, (expert_in, expert_grad, gate_weight, up_weight, down_weight))
    slot_out = slot_out.reshape(EXPERTS, groups, CAP, D).transpose(1, 0, 2, 3).reshape(groups, slots_all, D)
    slot_back = slot_back.reshape(EXPERTS, groups, CAP, D).transpose(1, 0, 2, 3).reshape(groups, slots_all, D)
    pair_out = jnp.take_along_axis(slot_out, slot_index[:, :, None], axis=1)
    pair_back = jnp.take_along_axis(slot_back, slot_index[:, :, None], axis=1)
    mixed = jnp.sum(pair_out.reshape(groups, TOK_GRP, TOP, D) * route_weights.reshape(groups, TOK_GRP, TOP, 1), axis=2)
    d_tokens = jnp.sum(pair_back.reshape(groups, TOK_GRP, TOP, D), axis=2)
    return mixed.reshape(TOKENS, D).astype(jnp.bfloat16), d_tokens.reshape(TOKENS, D).astype(jnp.bfloat16), d_down
```

```python
import jax
import jax.numpy as jnp
from jax import lax
from jax.sharding import Mesh, PartitionSpec as P

BF = jnp.bfloat16
F32 = jnp.float32
ETP = ("z", "xl")
CAPACITY = 8


def exchange(rows, axis):
    return lax.all_to_all(rows, axis, split_axis=0, concat_axis=0, tiled=True)


def shards(tokens, routes, route_weights, gate_weight, up_weight, down_weight, cotangent):
    local_experts, depth, hidden_width = gate_weight.shape
    groups = lax.axis_size("z") * lax.axis_size("xl")
    dp_size = lax.axis_size("y") * lax.axis_size("xh")
    num_experts = groups * local_experts
    tok_rows, top_count = routes.shape
    pairs = tok_rows * top_count
    slots_all = num_experts * CAPACITY
    half = depth // 2

    routes_flat = routes.reshape(pairs)
    expert_hot = (
        routes_flat[:, None] == jnp.arange(num_experts, dtype=jnp.int32)[None, :]
    ).astype(jnp.int32)
    position = jnp.sum((jnp.cumsum(expert_hot, axis=0) - 1) * expert_hot, axis=1)
    slot_index = (routes_flat * CAPACITY + position).reshape(tok_rows, top_count)

    slot_range = jnp.arange(slots_all, dtype=jnp.int32)
    hits = [slot_range[:, None] == slot_index[None, :, k] for k in range(top_count)]
    placing = sum(hit.astype(BF) for hit in hits)
    slot_weight = sum(
        jnp.sum(jnp.where(hit, route_weights[None, :, k], 0.0), axis=1)
        for k, hit in enumerate(hits)
    )
    sources = jnp.concatenate([tokens, cotangent], axis=1)
    placed = jnp.dot(placing, sources, preferred_element_type=F32)
    send = jnp.concatenate(
        [placed[:, :depth], placed[:, depth:] * slot_weight[:, None]], axis=1
    ).astype(BF)
    arrived = exchange(send, ETP)
    arrived = arrived.reshape(groups, local_experts, CAPACITY, 2 * depth)
    arrived = jnp.swapaxes(arrived, 0, 1).reshape(local_experts, groups * CAPACITY, 2 * depth)
    expert_in, expert_grad = arrived[..., :depth], arrived[..., depth:]

    terms = jnp.concatenate(
        [
            jnp.einsum("erd,edf->erf", expert_in, gate_weight, preferred_element_type=F32).astype(BF),
            jnp.einsum("erd,edf->erf", expert_in, up_weight, preferred_element_type=F32).astype(BF),
            jnp.einsum("erd,efd->erf", expert_grad, down_weight, preferred_element_type=F32).astype(BF),
        ],
        axis=2,
    )
    rows_all = local_experts * groups * CAPACITY
    terms = exchange(terms.reshape(rows_all, 3 * hidden_width), ("y", "xh"))
    sums = jnp.sum(
        terms.reshape(dp_size, rows_all // dp_size, 3 * hidden_width).astype(F32), axis=0
    )
    gate, up_proj, d_hidden = jnp.split(sums, 3, axis=1)
    sigmoid_gate = jax.nn.sigmoid(gate)
    silu_gate = gate * sigmoid_gate
    hidden = (silu_gate * up_proj).astype(BF)
    d_up = (d_hidden * silu_gate).astype(BF)
    d_gate = (d_hidden * up_proj * sigmoid_gate * (1.0 + gate * (1.0 - sigmoid_gate))).astype(BF)
    acts = jnp.concatenate([hidden, d_gate, d_up], axis=1)
    acts = lax.all_gather(acts, "xh", axis=0, tiled=True)
    acts = lax.all_gather(acts, "y", axis=0, tiled=True)
    acts = acts.reshape(local_experts, groups * CAPACITY, 3 * hidden_width)
    all_hidden, all_dgate, all_dup = jnp.split(acts, 3, axis=2)

    part_out = jnp.einsum(
        "erf,efd->erd", all_hidden, down_weight, preferred_element_type=F32
    ).astype(BF)
    part_grad = (
        jnp.einsum("erf,edf->erd", all_dgate, gate_weight, preferred_element_type=F32)
        + jnp.einsum("erf,edf->erd", all_dup, up_weight, preferred_element_type=F32)
    ).astype(BF)
    d_down = jnp.einsum(
        "erf,erd->efd", all_hidden, expert_grad, preferred_element_type=F32
    ).astype(BF)

    parts = jnp.stack(
        [
            jnp.concatenate([part_out[..., :half], part_grad[..., :half]], axis=2),
            jnp.concatenate([part_out[..., half:], part_grad[..., half:]], axis=2),
        ]
    )
    parts = lax.all_to_all(parts, "exp", split_axis=0, concat_axis=0, tiled=True)
    slot_sums = (parts[0].astype(F32) + parts[1].astype(F32)).astype(BF)
    slot_sums = slot_sums.reshape(local_experts, groups, CAPACITY, depth)
    slot_sums = jnp.swapaxes(slot_sums, 0, 1).reshape(slots_all, depth)
    back = exchange(slot_sums, ETP)

    picked = [
        jnp.dot(
            (slot_index[:, k, None] == slot_range[None, :]).astype(BF),
            back,
            preferred_element_type=F32,
        )
        for k in range(top_count)
    ]
    mixed = sum(p[:, :half] * route_weights[:, k, None] for k, p in enumerate(picked)).astype(BF)
    d_tokens = sum(p[:, half:] for p in picked).astype(BF)
    return mixed, d_tokens, d_down


def solution(mesh):
    fine = Mesh(mesh.devices.reshape(8, 2, 2, 8, 4), ("y", "xh", "exp", "z", "xl"))
    dp = ("y", "xh")
    in_specs = (
        P(ETP, dp),
        P(ETP, None),
        P(ETP, None),
        P(ETP, dp, "exp"),
        P(ETP, dp, "exp"),
        P(ETP, "exp", dp),
        P(ETP, dp),
    )
    out_specs = (P(ETP, dp + ("exp",)), P(ETP, dp + ("exp",)), P(ETP, "exp", dp))
    return jax.shard_map(shards, mesh=fine, in_specs=in_specs, out_specs=out_specs, check_vma=False)
```

```python
import jax
import jax.numpy as jnp
from jax import lax
from jax.sharding import Mesh, PartitionSpec as P

BF = jnp.bfloat16
F32 = jnp.float32
ETP = ("z", "xl")
CAPACITY = 8


def exchange(rows, axis):
    return lax.all_to_all(rows, axis, split_axis=0, concat_axis=0, tiled=True)


def step(block, axis, shift):
    size = lax.axis_size(axis)
    return lax.ppermute(block, axis, [(i, (i + shift) % size) for i in range(size)])


def ring_sum(terms, rows):
    size = lax.axis_size("y")
    mine = lax.axis_index("y")
    far, half = size // 2, rows // 2

    def own(offset, start, count):
        chunk = lax.rem(mine + offset + size, size)
        return lax.dynamic_slice_in_dim(terms, chunk * rows + start, count, 0)

    up = step(own(far, 0, half).astype(BF), "y", 1)
    down = step(own(-far, half, half).astype(BF), "y", -1)
    up = jnp.concatenate(
        [own(far - 1, 0, half) + up.astype(F32), own(far - 1, half, half)], axis=0
    ).astype(BF)
    down = jnp.concatenate(
        [own(1 - far, 0, half), own(1 - far, half, half) + down.astype(F32)], axis=0
    ).astype(BF)
    for distance in range(far - 2, -1, -1):
        up, down = step(up, "y", 1), step(down, "y", -1)
        if distance > 0:
            up = (own(distance, 0, rows) + up.astype(F32)).astype(BF)
            down = (own(-distance, 0, rows) + down.astype(F32)).astype(BF)
    return own(0, 0, rows) + (up.astype(F32) + down.astype(F32))


def ring_gather(block):
    size = lax.axis_size("y")
    mine = lax.axis_index("y")
    rows = block.shape[0]
    far, half = size // 2, rows // 2
    whole = jnp.zeros((size * rows, block.shape[1]), block.dtype)

    def put(whole, piece, offset, start):
        chunk = lax.rem(mine + offset + size, size)
        return lax.dynamic_update_slice_in_dim(whole, piece, chunk * rows + start, 0)

    whole = put(whole, block, 0, 0)
    up = down = block
    for distance in range(1, far):
        up, down = step(up, "y", 1), step(down, "y", -1)
        whole = put(put(whole, up, -distance, 0), down, distance, 0)
    up, down = step(up[:half], "y", 1), step(down[half:], "y", -1)
    return put(put(whole, up, far, 0), down, far, half)


def shards(tokens, routes, route_weights, gate_weight, up_weight, down_weight, cotangent):
    local_experts, depth, hidden_width = gate_weight.shape
    groups = lax.axis_size("z") * lax.axis_size("xl")
    num_experts = groups * local_experts
    tok_rows, top_count = routes.shape
    pairs = tok_rows * top_count
    slots_all = num_experts * CAPACITY
    half = depth // 2
    core = lax.axis_index("exp")

    routes_flat = routes.reshape(pairs)
    expert_hot = (
        routes_flat[:, None] == jnp.arange(num_experts, dtype=jnp.int32)[None, :]
    ).astype(jnp.int32)
    position = jnp.sum((jnp.cumsum(expert_hot, axis=0) - 1) * expert_hot, axis=1)
    slot_index = (routes_flat * CAPACITY + position).reshape(tok_rows, top_count)

    slot_range = jnp.arange(slots_all, dtype=jnp.int32)
    hits = [slot_range[:, None] == slot_index[None, :, k] for k in range(top_count)]
    placing = sum(hit.astype(BF) for hit in hits)
    slot_weight = sum(
        jnp.sum(jnp.where(hit, route_weights[None, :, k], 0.0), axis=1)
        for k, hit in enumerate(hits)
    )
    source = jnp.where(core == 0, tokens, cotangent)
    scale = jnp.where(core == 0, 1.0, slot_weight)
    send = (jnp.dot(placing, source, preferred_element_type=F32) * scale[:, None]).astype(BF)
    arrived = exchange(send, ETP).reshape(groups, local_experts, CAPACITY, depth)
    arrived = jnp.swapaxes(arrived, 0, 1).reshape(slots_all, depth)
    arrived = lax.all_gather(arrived, "exp", axis=0, tiled=True)
    arrived = arrived.reshape(2, local_experts, groups * CAPACITY, depth)
    expert_in, expert_grad = arrived[0], arrived[1]

    terms = jnp.concatenate(
        [
            jnp.einsum("erd,edf->erf", expert_in, gate_weight, preferred_element_type=F32),
            jnp.einsum("erd,edf->erf", expert_in, up_weight, preferred_element_type=F32),
            jnp.einsum("erd,efd->erf", expert_grad, down_weight, preferred_element_type=F32),
        ],
        axis=2,
    ).reshape(slots_all, 3 * hidden_width)
    sums = ring_sum(terms, slots_all // lax.axis_size("y"))
    sums = sums + step(sums.astype(BF), "xh", 1).astype(F32)
    gate, up_proj, d_hidden = jnp.split(sums, 3, axis=1)
    sigmoid_gate = jax.nn.sigmoid(gate)
    silu_gate = gate * sigmoid_gate
    hidden = (silu_gate * up_proj).astype(BF)
    d_up = (d_hidden * silu_gate).astype(BF)
    d_gate = (d_hidden * up_proj * sigmoid_gate * (1.0 + gate * (1.0 - sigmoid_gate))).astype(BF)
    acts = ring_gather(jnp.concatenate([hidden, d_gate, d_up], axis=1))
    acts = acts.reshape(local_experts, groups * CAPACITY, 3 * hidden_width)
    all_hidden, all_dgate, all_dup = jnp.split(acts, 3, axis=2)

    part_out = jnp.einsum(
        "erf,efd->erd", all_hidden, down_weight, preferred_element_type=F32
    ).astype(BF)
    part_grad = (
        jnp.einsum("erf,edf->erd", all_dgate, gate_weight, preferred_element_type=F32)
        + jnp.einsum("erf,edf->erd", all_dup, up_weight, preferred_element_type=F32)
    ).astype(BF)
    d_down = jnp.einsum(
        "erf,erd->efd", all_hidden, expert_grad, preferred_element_type=F32
    ).astype(BF)

    parts = jnp.stack(
        [
            jnp.concatenate([part_out[..., :half], part_grad[..., :half]], axis=2),
            jnp.concatenate([part_out[..., half:], part_grad[..., half:]], axis=2),
        ]
    )
    parts = lax.all_to_all(parts, "exp", split_axis=0, concat_axis=0, tiled=True)
    slot_sums = (parts[0].astype(F32) + parts[1].astype(F32)).astype(BF)
    slot_sums = slot_sums.reshape(local_experts, groups, CAPACITY, depth)
    slot_sums = jnp.swapaxes(slot_sums, 0, 1).reshape(slots_all, depth)
    back = exchange(slot_sums, ETP)

    picked = [
        jnp.dot(
            (slot_index[:, k, None] == slot_range[None, :]).astype(BF),
            back,
            preferred_element_type=F32,
        )
        for k in range(top_count)
    ]
    mixed = sum(p[:, :half] * route_weights[:, k, None] for k, p in enumerate(picked)).astype(BF)
    d_tokens = sum(p[:, half:] for p in picked).astype(BF)
    return mixed, d_tokens, d_down


def solution(mesh):
    fine = Mesh(mesh.devices.reshape(8, 2, 2, 8, 4), ("y", "xh", "exp", "z", "xl"))
    dp = ("y", "xh")
    in_specs = (
        P(ETP, dp),
        P(ETP, None),
        P(ETP, None),
        P(ETP, dp, "exp"),
        P(ETP, dp, "exp"),
        P(ETP, "exp", dp),
        P(ETP, dp),
    )
    out_specs = (P(ETP, dp + ("exp",)), P(ETP, dp + ("exp",)), P(ETP, "exp", dp))
    return jax.shard_map(shards, mesh=fine, in_specs=in_specs, out_specs=out_specs, check_vma=False)
```

```python
import functools

import jax
import jax.numpy as jnp
from jax import lax
from jax.experimental import pallas as pl
from jax.experimental.pallas import tpu as pltpu
from jax.sharding import Mesh, PartitionSpec as P

BF = jnp.bfloat16
F32 = jnp.float32
ETP = ("z", "xl")
CAPACITY = 8
VMEM = pl.BlockSpec(memory_space=pltpu.VMEM)
SMEM = pl.BlockSpec(memory_space=pltpu.SMEM)
LIMIT = pltpu.CompilerParams(vmem_limit_bytes=40 * 1024 * 1024)
NT = (((1,), (1,)), ((), ()))


def call(kernel, outs, *args, scalars=0, scratch=()):
    return pl.pallas_call(
        kernel,
        out_shape=outs,
        in_specs=[SMEM] * scalars + [VMEM] * (len(args) - scalars),
        out_specs=jax.tree.map(lambda _: VMEM, outs),
        scratch_shapes=scratch,
        compiler_params=LIMIT,
    )(*args)


def shape(dims, kind):
    return jax.ShapeDtypeStruct(dims, kind)


def iota(dims, axis):
    return lax.broadcasted_iota(jnp.int32, dims, axis)


def place_rows(experts, core_ref, routes_ref, weights_ref, tokens_ref, cot_ref, send_ref, slot_ref):
    top_count, tok_rows = routes_ref.shape
    hots = [iota((experts, tok_rows), 0) == routes_ref[k : k + 1, :] for k in range(top_count)]
    both = sum(jnp.where(hot, 1.0, 0.0) for hot in hots)
    earlier = jnp.where(iota((tok_rows, tok_rows), 0) < iota((tok_rows, tok_rows), 1), 1.0, 0.0)
    count = jnp.dot(both.astype(BF), earlier.astype(BF), preferred_element_type=F32)
    placing = jnp.zeros((send_ref.shape[0], tok_rows), F32)
    slot_weight = jnp.zeros((send_ref.shape[0], 1), F32)
    for k, hot in enumerate(hots):
        position = jnp.sum(jnp.where(hot, count, 0.0), axis=0, keepdims=True).astype(jnp.int32)
        slot = routes_ref[k : k + 1, :] * CAPACITY + position
        slot_ref[k : k + 1, :] = slot
        hit = iota(placing.shape, 0) == slot
        placing = placing + jnp.where(hit, 1.0, 0.0)
        slot_weight = slot_weight + jnp.sum(
            jnp.where(hit, weights_ref[k : k + 1, :], 0.0), axis=1, keepdims=True
        )
    first = core_ref[0] == 0
    source = jnp.where(first, tokens_ref[...].astype(F32), cot_ref[...].astype(F32)).astype(BF)
    scale = jnp.where(first, 1.0, slot_weight)
    rows = jnp.dot(placing.astype(BF), source, preferred_element_type=F32)
    send_ref[...] = (rows * scale).astype(BF)


def first_terms(mine_ref, rows_ref, gate_ref, up_ref, down_ref, terms_ref, grad_ref, up_msg, down_msg):
    local_experts, depth, width = gate_ref.shape
    slots = rows_ref.shape[0] // 2
    groups = slots // (local_experts * CAPACITY)
    kinds = []
    for kind in range(2):
        rows = rows_ref[kind * slots : (kind + 1) * slots, :].astype(F32)
        kinds.append(rows.reshape(groups, local_experts, CAPACITY, depth))
    count = groups * CAPACITY
    for e in range(local_experts):
        rows_in = kinds[0][:, e].reshape(count, depth).astype(BF)
        rows_grad = kinds[1][:, e].reshape(count, depth).astype(BF)
        here = slice(e * count, (e + 1) * count)
        terms_ref[here, :width] = jnp.dot(rows_in, gate_ref[e], preferred_element_type=F32)
        terms_ref[here, width : 2 * width] = jnp.dot(rows_in, up_ref[e], preferred_element_type=F32)
        terms_ref[here, 2 * width :] = lax.dot_general(
            rows_grad, down_ref[e], NT, preferred_element_type=F32
        )
        grad_ref[e] = rows_grad
    half = up_msg.shape[0]
    chunk = lax.rem(mine_ref[0] + 4, 8)
    base = pl.multiple_of(chunk * 2 * half, 2 * half)
    up_msg[...] = terms_ref[pl.ds(base, half), :].astype(BF)
    down_msg[...] = terms_ref[pl.ds(base + half, half), :].astype(BF)


def add_terms(distance, mine_ref, terms_ref, up_ref, down_ref, up_msg, down_msg):
    rows = up_msg.shape[0]
    for offset, came, out in ((distance, up_ref, up_msg), (-distance, down_ref, down_msg)):
        chunk = lax.rem(mine_ref[0] + (offset + 8), 8)
        base = pl.multiple_of(chunk * rows, rows)
        if came.shape[0] == rows:
            out[...] = (terms_ref[pl.ds(base, rows), :] + came[...].astype(F32)).astype(BF)
        else:
            half = rows // 2
            for part, has in ((0, offset > 0), (half, offset < 0)):
                own = terms_ref[pl.ds(base + part, half), :]
                own = own + came[...].astype(F32) if has else own
                out[part : part + half, :] = own.astype(BF)


def end_terms(mine_ref, terms_ref, up_ref, down_ref, out_ref):
    rows = out_ref.shape[0]
    base = pl.multiple_of(mine_ref[0] * rows, rows)
    came = up_ref[...].astype(F32) + down_ref[...].astype(F32)
    out_ref[...] = (terms_ref[pl.ds(base, rows), :] + came).astype(BF)


def activate(pair_ref, out_ref):
    rows, width = out_ref.shape[0], out_ref.shape[1] // 3
    low, high = slice(0, rows), slice(rows, 2 * rows)

    def total(part):
        cols = slice(part * width, (part + 1) * width)
        return pair_ref[low, cols].astype(F32) + pair_ref[high, cols].astype(F32)

    gate, up_proj, d_hidden = total(0), total(1), total(2)
    sigmoid_gate = jax.nn.sigmoid(gate)
    silu_gate = gate * sigmoid_gate
    out_ref[:, :width] = (silu_gate * up_proj).astype(BF)
    out_ref[:, width : 2 * width] = (
        d_hidden * up_proj * sigmoid_gate * (1.0 + gate * (1.0 - sigmoid_gate))
    ).astype(BF)
    out_ref[:, 2 * width :] = (d_hidden * silu_gate).astype(BF)


def last_terms(pieces, mine_ref, *refs):
    piece_refs = refs[: len(pieces)]
    gate_ref, up_ref, down_ref, parts_ref, hidden_ref, acts = refs[len(pieces) :]
    local_experts, depth, width = gate_ref.shape
    rows = acts.shape[0] // 8
    for (offset, start), piece in zip(pieces, piece_refs):
        chunk = lax.rem(mine_ref[0] + (offset + 8), 8)
        base = pl.multiple_of(chunk * rows, rows) + start
        acts[pl.ds(pl.multiple_of(base, rows // 2), piece.shape[0]), :] = piece[...]
    count = acts.shape[0] // local_experts
    outs, grads = [], []
    for e in range(local_experts):
        here = slice(e * count, (e + 1) * count)
        hidden = acts[here, :width]
        hidden_ref[e] = hidden
        out = jnp.dot(hidden, down_ref[e], preferred_element_type=F32)
        grad = lax.dot_general(
            acts[here, width : 2 * width], gate_ref[e], NT, preferred_element_type=F32
        ) + lax.dot_general(acts[here, 2 * width :], up_ref[e], NT, preferred_element_type=F32)
        outs.append(out.reshape(count // CAPACITY, CAPACITY, depth))
        grads.append(grad.reshape(count // CAPACITY, CAPACITY, depth))
    out, grad = jnp.concatenate(outs, axis=1), jnp.concatenate(grads, axis=1)
    half = depth // 2
    for j in range(2):
        cols = slice(j * half, (j + 1) * half)
        parts_ref[j, :, :, :half] = out[:, :, cols].astype(BF)
        parts_ref[j, :, :, half:] = grad[:, :, cols].astype(BF)


def combine(slot_ref, weights_ref, back_ref, mixed_ref, grads_ref):
    top_count, tok_rows = slot_ref.shape
    slots, width = back_ref.shape[0] // 2, back_ref.shape[1]
    half = width // 2
    same = iota((tok_rows, tok_rows), 0) == iota((tok_rows, tok_rows), 1)

    def column(row):
        return jnp.sum(jnp.where(same, row, 0.0), axis=1, keepdims=True)

    mixed = jnp.zeros((tok_rows, half), F32)
    grads = jnp.zeros((tok_rows, half), F32)
    for k in range(top_count):
        slot = column(slot_ref[k : k + 1, :].astype(F32)).astype(jnp.int32)
        hot = jnp.where(iota((tok_rows, slots), 1) == slot, 1.0, 0.0).astype(BF)
        picked = jnp.dot(hot, back_ref[:slots, :], preferred_element_type=F32) + jnp.dot(
            hot, back_ref[slots:, :], preferred_element_type=F32
        )
        mixed = mixed + picked[:, :half] * column(weights_ref[k : k + 1, :])
        grads = grads + picked[:, half:]
    mixed_ref[...] = mixed.astype(BF)
    grads_ref[...] = grads.astype(BF)


def exchange(rows, axis):
    return lax.all_to_all(rows, axis, split_axis=0, concat_axis=0, tiled=True)


def step(block, axis, shift):
    size = lax.axis_size(axis)
    return lax.ppermute(block, axis, [(i, (i + shift) % size) for i in range(size)])


def both_ways(up, down):
    return step(up, "y", 1), step(down, "y", -1)


def shards(tokens, routes, route_weights, gate_weight, up_weight, down_weight, cotangent):
    local_experts, depth, width = gate_weight.shape
    groups = lax.axis_size("z") * lax.axis_size("xl")
    experts = groups * local_experts
    tok_rows, top_count = routes.shape
    slots = experts * CAPACITY
    chunk = slots // 8
    core = lax.axis_index("exp").reshape(1)
    mine = lax.axis_index("y").reshape(1)
    routes, route_weights = routes.T, route_weights.T

    send, slot_index = call(
        functools.partial(place_rows, experts),
        (shape((slots, depth), BF), shape((top_count, tok_rows), jnp.int32)),
        core, routes, route_weights, tokens, cotangent, scalars=1,
    )
    arrived = lax.all_gather(exchange(send, ETP), "exp", axis=0, tiled=True)

    block = shape((chunk, 3 * width), BF)
    half_block = shape((chunk // 2, 3 * width), BF)
    terms, expert_grad, up, down = call(
        first_terms,
        (
            shape((slots, 3 * width), F32),
            shape((local_experts, groups * CAPACITY, depth), BF),
            half_block, half_block,
        ),
        mine, arrived, gate_weight, up_weight, down_weight, scalars=1,
    )
    for distance in (3, 2, 1):
        up, down = both_ways(up, down)
        up, down = call(
            functools.partial(add_terms, distance), (block, block), mine, terms, up, down, scalars=1
        )
    up, down = both_ways(up, down)
    sums = call(end_terms, block, mine, terms, up, down, scalars=1)
    acts = call(activate, block, lax.all_gather(sums, "xh", axis=0, tiled=True))

    pieces, values = [(0, 0)], [acts]
    up = down = acts
    for distance in (1, 2, 3):
        up, down = both_ways(up, down)
        pieces += [(-distance, 0), (distance, 0)]
        values += [up, down]
    pieces += [(4, 0), (4, chunk // 2)]
    values += both_ways(up[: chunk // 2], down[chunk // 2 :])
    parts, hidden = call(
        functools.partial(last_terms, pieces),
        (
            shape((2, groups, local_experts * CAPACITY, depth), BF),
            shape((local_experts, groups * CAPACITY, width), BF),
        ),
        mine, *values, gate_weight, up_weight, down_weight, scalars=1,
        scratch=[pltpu.VMEM((slots, 3 * width), BF)],
    )
    d_down = jnp.einsum("erf,erd->efd", hidden, expert_grad, preferred_element_type=F32).astype(BF)
    back = exchange(parts.reshape(2 * slots, depth), ("exp",) + ETP)
    mixed, d_tokens = call(
        combine,
        (shape((tok_rows, depth // 2), BF), shape((tok_rows, depth // 2), BF)),
        slot_index, route_weights, back,
    )
    return mixed, d_tokens, d_down


def solution(mesh):
    fine = Mesh(mesh.devices.reshape(8, 2, 2, 8, 4), ("y", "xh", "exp", "z", "xl"))
    dp = ("y", "xh")
    in_specs = (
        P(ETP, dp),
        P(ETP, None),
        P(ETP, None),
        P(ETP, dp, "exp"),
        P(ETP, dp, "exp"),
        P(ETP, "exp", dp),
        P(ETP, dp),
    )
    out_specs = (P(ETP, dp + ("exp",)), P(ETP, dp + ("exp",)), P(ETP, "exp", dp))
    return jax.shard_map(shards, mesh=fine, in_specs=in_specs, out_specs=out_specs, check_vma=False)
```

```python
import functools

import jax
import jax.numpy as jnp
from jax import lax
from jax.experimental import pallas as pl
from jax.experimental.pallas import tpu as pltpu
from jax.sharding import Mesh, PartitionSpec as P

BF = jnp.bfloat16
F32 = jnp.float32
ETP = ("z", "xl")
CAPACITY = 8
VMEM = pl.BlockSpec(memory_space=pltpu.VMEM)
SMEM = pl.BlockSpec(memory_space=pltpu.SMEM)
LIMIT = pltpu.CompilerParams(vmem_limit_bytes=40 * 1024 * 1024)
NT = (((1,), (1,)), ((), ()))
TN = (((0,), (0,)), ((), ()))


def call(kernel, outs, *args, scalars=0, given=0):
    rest = len(args) - scalars - given
    return pl.pallas_call(
        kernel,
        out_shape=outs,
        in_specs=[SMEM] * scalars + [pl.BlockSpec()] * given + [VMEM] * rest,
        out_specs=jax.tree.map(lambda _: VMEM, outs),
        compiler_params=LIMIT,
    )(*args)


def shape(dims, kind):
    return jax.ShapeDtypeStruct(dims, kind)


def iota(dims, axis):
    return lax.broadcasted_iota(jnp.int32, dims, axis)


def begin(experts, core_ref, member_ref, routes_ref, weights_ref, tokens_ref, cot_ref,
          gate_ref, up_ref, down_ref, send_ref, slot_ref, kept_ref, given_ref):
    local_experts, _, width = gate_ref.shape
    half = width // 2
    for out, member in ((given_ref, 1 - member_ref[0]), (kept_ref, member_ref[0])):
        units = pl.ds(pl.multiple_of(member * half, 128), half)
        for e in range(local_experts):
            out[e, :, :half] = gate_ref[e, :, units]
            out[e, :, half : 2 * half] = up_ref[e, :, units]
            out[e, :, 2 * half :] = down_ref[e, units, :].T
    top_count, tok_rows = routes_ref.shape
    hots = [iota((experts, tok_rows), 0) == routes_ref[k : k + 1, :] for k in range(top_count)]
    both = sum(jnp.where(hot, 1.0, 0.0) for hot in hots)
    earlier = jnp.where(iota((tok_rows, tok_rows), 0) < iota((tok_rows, tok_rows), 1), 1.0, 0.0)
    count = jnp.dot(both.astype(BF), earlier.astype(BF), preferred_element_type=F32)
    placing = jnp.zeros((send_ref.shape[0], tok_rows), F32)
    slot_weight = jnp.zeros((send_ref.shape[0], 1), F32)
    for k, hot in enumerate(hots):
        position = jnp.sum(jnp.where(hot, count, 0.0), axis=0, keepdims=True).astype(jnp.int32)
        slot = routes_ref[k : k + 1, :] * CAPACITY + position
        slot_ref[k : k + 1, :] = slot
        hit = iota(placing.shape, 0) == slot
        placing = placing + jnp.where(hit, 1.0, 0.0)
        slot_weight = slot_weight + jnp.sum(
            jnp.where(hit, weights_ref[k : k + 1, :], 0.0), axis=1, keepdims=True
        )
    first = core_ref[0] == 0
    source = jnp.where(first, tokens_ref[...].astype(F32), cot_ref[...].astype(F32)).astype(BF)
    scale = jnp.where(first, 1.0, slot_weight)
    rows = jnp.dot(placing.astype(BF), source, preferred_element_type=F32)
    send_ref[...] = (rows * scale).astype(BF)


def first_terms(kept_ref, other_ref, rows_ref, other_rows_ref, terms_ref, grad_ref, other_grad_ref):
    local_experts, depth, width = kept_ref.shape
    two = width // 3 * 2
    slots = rows_ref.shape[0] // 2
    count = slots // local_experts
    for e in range(local_experts):
        here = slice(e * count, (e + 1) * count)
        totals = [0.0, 0.0]
        for weights, rows, grads in (
            (kept_ref, rows_ref, grad_ref), (other_ref, other_rows_ref, other_grad_ref)
        ):
            for kind, cols in enumerate((slice(0, two), slice(two, width))):
                picked = rows[kind * slots : (kind + 1) * slots, :].astype(F32)
                picked = picked.reshape(-1, local_experts, CAPACITY, depth)[:, e]
                picked = picked.reshape(count, depth).astype(BF)
                totals[kind] += jnp.dot(picked, weights[e, :, cols], preferred_element_type=F32)
                if kind == 1:
                    grads[e] = picked
        terms_ref[here, :two] = totals[0].astype(BF)
        terms_ref[here, two:] = totals[1].astype(BF)


def activate(terms_ref, out_ref):
    copies, rows, width = out_ref.shape
    width = width // 3

    def total(part):
        cols = slice(part * width, (part + 1) * width)
        return sum(terms_ref[i, :, cols].astype(F32) for i in range(terms_ref.shape[0]))

    gate, up_proj, d_hidden = total(0), total(1), total(2)
    sigmoid_gate = jax.nn.sigmoid(gate)
    silu_gate = gate * sigmoid_gate
    hidden = (silu_gate * up_proj).astype(BF)
    d_gate = (d_hidden * up_proj * sigmoid_gate * (1.0 + gate * (1.0 - sigmoid_gate))).astype(BF)
    d_up = (d_hidden * silu_gate).astype(BF)
    for i in range(copies):
        out_ref[i, :, :width] = hidden
        out_ref[i, :, width : 2 * width] = d_gate
        out_ref[i, :, 2 * width :] = d_up


def last_terms(member_ref, acts_ref, kept_ref, other_ref, parts_ref):
    local_experts, depth, width = kept_ref.shape
    one = width // 3
    count = acts_ref.shape[0] // local_experts
    half = depth // 2
    for weights, member in ((kept_ref, member_ref[0]), (other_ref, 1 - member_ref[0])):
        outs, grads = [], []
        for e in range(local_experts):
            here = slice(e * count, (e + 1) * count)
            out = lax.dot_general(
                acts_ref[here, :one], weights[e, :, 2 * one :], NT, preferred_element_type=F32
            )
            grad = lax.dot_general(
                acts_ref[here, one:], weights[e, :, : 2 * one], NT, preferred_element_type=F32
            )
            outs.append(out.reshape(count // CAPACITY, CAPACITY, depth))
            grads.append(grad.reshape(count // CAPACITY, CAPACITY, depth))
        out, grad = jnp.concatenate(outs, axis=1), jnp.concatenate(grads, axis=1)
        for j in range(2):
            cols = slice(j * half, (j + 1) * half)
            parts_ref[member * 2 + j, :, :, :half] = out[:, :, cols].astype(BF)
            parts_ref[member * 2 + j, :, :, half:] = grad[:, :, cols].astype(BF)


def down_terms(acts_ref, grad_ref, other_grad_ref, out_ref, other_out_ref):
    local_experts, count, _ = grad_ref.shape
    one = out_ref.shape[1]
    for e in range(local_experts):
        hidden = acts_ref[e * count : (e + 1) * count, :one]
        for grads, out in ((grad_ref, out_ref), (other_grad_ref, other_out_ref)):
            out[e] = lax.dot_general(hidden, grads[e], TN, preferred_element_type=F32).astype(BF)


def add_parts(parts_ref, out_ref):
    out_ref[...] = sum(parts_ref[i].astype(F32) for i in range(parts_ref.shape[0])).astype(BF)


def combine(slot_ref, weights_ref, back_ref, mixed_ref, grads_ref):
    top_count, tok_rows = slot_ref.shape
    slots, width = back_ref.shape
    half = width // 2
    same = iota((tok_rows, tok_rows), 0) == iota((tok_rows, tok_rows), 1)

    def column(row):
        return jnp.sum(jnp.where(same, row, 0.0), axis=1, keepdims=True)

    mixed = jnp.zeros((tok_rows, half), F32)
    grads = jnp.zeros((tok_rows, half), F32)
    for k in range(top_count):
        slot = column(slot_ref[k : k + 1, :].astype(F32)).astype(jnp.int32)
        hot = jnp.where(iota((tok_rows, slots), 1) == slot, 1.0, 0.0).astype(BF)
        picked = jnp.dot(hot, back_ref[...], preferred_element_type=F32)
        mixed = mixed + picked[:, :half] * column(weights_ref[k : k + 1, :])
        grads = grads + picked[:, half:]
    mixed_ref[...] = mixed.astype(BF)
    grads_ref[...] = grads.astype(BF)


def exchange(rows, axis):
    return lax.all_to_all(rows, axis, split_axis=0, concat_axis=0, tiled=True)


def swap(block):
    return lax.ppermute(block, "ym", [(0, 1), (1, 0)])


def shards(tokens, routes, route_weights, gate_weight, up_weight, down_weight, cotangent):
    local_experts, depth, width = gate_weight.shape
    groups = lax.axis_size("z") * lax.axis_size("xl")
    experts = groups * local_experts
    tok_rows, top_count = routes.shape
    slots = experts * CAPACITY
    count = groups * CAPACITY
    half = width // 2
    slices = lax.axis_size("yp") * lax.axis_size("xh")
    core = lax.axis_index("exp").reshape(1)
    member = lax.axis_index("ym").reshape(1)
    routes, route_weights = routes.T, route_weights.T

    weights = shape((local_experts, depth, 3 * half), BF)
    send, slot_index, kept, given = call(
        functools.partial(begin, experts),
        (shape((slots, depth), BF), shape((top_count, tok_rows), jnp.int32), weights, weights),
        core, member, routes, route_weights, tokens, cotangent, gate_weight, up_weight,
        down_weight, scalars=2, given=7,
    )
    other = swap(given)
    arrived = exchange(send, ETP)
    other_arrived = swap(arrived)
    rows = lax.all_gather(arrived, "exp", axis=0, tiled=True)
    other_rows = lax.all_gather(other_arrived, "exp", axis=0, tiled=True)

    grads = shape((local_experts, count, depth), BF)
    terms, expert_grad, other_grad = call(
        first_terms, (shape((slots, 3 * half), BF), grads, grads), kept, other, rows, other_rows
    )
    terms = exchange(terms, ("yp", "xh")).reshape(slices, slots // slices, 3 * half)
    acts = call(activate, shape(terms.shape, BF), terms)
    acts = exchange(acts.reshape(slots, 3 * half), ("yp", "xh"))

    parts = call(
        last_terms, shape((4, groups, local_experts * CAPACITY, depth), BF),
        member, acts, kept, other, scalars=1,
    )
    parts = exchange(parts.reshape(4 * slots, depth), ("ym", "exp")).reshape(4, slots, depth)
    slot_sums = call(add_parts, shape((slots, depth), BF), parts)
    back = exchange(slot_sums, ETP)
    downs = shape((local_experts, half, depth), BF)
    d_down, other_down = call(down_terms, (downs, downs), acts, expert_grad, other_grad)
    other_down = swap(other_down)
    first = member[0] == 0
    d_down = jnp.concatenate(
        [jnp.where(first, d_down, other_down), jnp.where(first, other_down, d_down)], axis=1
    )
    mixed, d_tokens = call(
        combine,
        (shape((tok_rows, depth // 2), BF), shape((tok_rows, depth // 2), BF)),
        slot_index, route_weights, back,
    )
    return mixed, d_tokens, d_down


def solution(mesh):
    fine = Mesh(mesh.devices.reshape(4, 2, 2, 2, 8, 4), ("yp", "ym", "xh", "exp", "z", "xl"))
    dp = ("yp", "ym", "xh")
    in_specs = (
        P(ETP, dp),
        P(ETP, None),
        P(ETP, None),
        P(ETP, dp, "exp"),
        P(ETP, dp, "exp"),
        P(ETP, "exp", dp),
        P(ETP, dp),
    )
    out_specs = (P(ETP, dp + ("exp",)), P(ETP, dp + ("exp",)), P(ETP, "exp", dp))
    return jax.shard_map(shards, mesh=fine, in_specs=in_specs, out_specs=out_specs, check_vma=False)
```

```python
import functools

import jax
import jax.numpy as jnp
from jax import lax
from jax.experimental import pallas as pl
from jax.experimental.pallas import tpu as pltpu
from jax.sharding import Mesh, PartitionSpec as P

BF = jnp.bfloat16
F32 = jnp.float32
ETP = ("z", "xl")
CAPACITY = 8
VMEM = pl.BlockSpec(memory_space=pltpu.VMEM)
SMEM = pl.BlockSpec(memory_space=pltpu.SMEM)
HBM = pl.BlockSpec(memory_space=pltpu.HBM)
LIMIT = pltpu.CompilerParams(vmem_limit_bytes=40 * 1024 * 1024)
NT = (((1,), (1,)), ((), ()))
TN = (((0,), (0,)), ((), ()))


def call(kernel, outs, *args, scalars=0, given=0, scratch=()):
    rest = len(args) - scalars - given
    return pl.pallas_call(
        kernel,
        out_shape=outs,
        in_specs=[SMEM] * scalars + [HBM] * given + [VMEM] * rest,
        out_specs=jax.tree.map(lambda _: VMEM, outs),
        scratch_shapes=scratch,
        compiler_params=pltpu.CompilerParams(vmem_limit_bytes=(56 if given else 40) * 1024 * 1024),
    )(*args)


def shape(dims, kind):
    return jax.ShapeDtypeStruct(dims, kind)


def iota(dims, axis):
    return lax.broadcasted_iota(jnp.int32, dims, axis)


def pack(member_ref, gate_hbm, up_hbm, down_hbm, kept_ref, given_ref, down, sems):
    local_experts, _, width = kept_ref.shape
    half = width // 3
    copies = [pltpu.make_async_copy(down_hbm, down, sems.at[0])]
    sides = ((given_ref, 1 - member_ref[0]), (kept_ref, member_ref[0]))
    for i, (out, member) in enumerate(sides):
        units = pl.ds(pl.multiple_of(member * half, 128), half)
        for j, weights in enumerate((gate_hbm, up_hbm)):
            copies.append(
                pltpu.make_async_copy(
                    weights.at[:, :, units],
                    out.at[:, :, j * half : (j + 1) * half],
                    sems.at[1 + 2 * i + j],
                )
            )
    for copy in copies:
        copy.start()
    copies[0].wait()
    for out, member in sides:
        units = pl.ds(pl.multiple_of(member * half, 128), half)
        for e in range(local_experts):
            out[e, :, 2 * half :] = down[e, units, :].T
    for copy in copies[1:]:
        copy.wait()


def place_rows(experts, core_ref, routes_hbm, weights_hbm, tokens_hbm, cot_hbm, send_ref, slot_ref,
               routes_ref, weights_ref, tokens_ref, cot_ref, sems):
    copies = [
        pltpu.make_async_copy(source, target, sems.at[i])
        for i, (source, target) in enumerate(
            (
                (routes_hbm, routes_ref), (weights_hbm, weights_ref),
                (tokens_hbm, tokens_ref), (cot_hbm, cot_ref),
            )
        )
    ]
    for copy in copies:
        copy.start()
    for copy in copies[:2]:
        copy.wait()
    top_count, tok_rows = routes_ref.shape
    hots = [iota((experts, tok_rows), 0) == routes_ref[k : k + 1, :] for k in range(top_count)]
    both = sum(jnp.where(hot, 1.0, 0.0) for hot in hots)
    earlier = jnp.where(iota((tok_rows, tok_rows), 0) < iota((tok_rows, tok_rows), 1), 1.0, 0.0)
    count = jnp.dot(both.astype(BF), earlier.astype(BF), preferred_element_type=F32)
    placing = jnp.zeros((send_ref.shape[0], tok_rows), F32)
    slot_weight = jnp.zeros((send_ref.shape[0], 1), F32)
    for k, hot in enumerate(hots):
        position = jnp.sum(jnp.where(hot, count, 0.0), axis=0, keepdims=True).astype(jnp.int32)
        slot = routes_ref[k : k + 1, :] * CAPACITY + position
        slot_ref[k : k + 1, :] = slot
        hit = iota(placing.shape, 0) == slot
        placing = placing + jnp.where(hit, 1.0, 0.0)
        slot_weight = slot_weight + jnp.sum(
            jnp.where(hit, weights_ref[k : k + 1, :], 0.0), axis=1, keepdims=True
        )
    for copy in copies[2:]:
        copy.wait()
    first = core_ref[0] == 0
    source = jnp.where(first, tokens_ref[...].astype(F32), cot_ref[...].astype(F32)).astype(BF)
    scale = jnp.where(first, 1.0, slot_weight)
    rows = jnp.dot(placing.astype(BF), source, preferred_element_type=F32)
    send_ref[...] = (rows * scale).astype(BF)


def first_terms(kept_ref, other_ref, rows_ref, other_rows_ref, terms_ref, grad_ref, other_grad_ref):
    local_experts, depth, width = kept_ref.shape
    two = width // 3 * 2
    slots = rows_ref.shape[0] // 2
    count = slots // local_experts
    for e in range(local_experts):
        here = slice(e * count, (e + 1) * count)
        totals = [0.0, 0.0]
        for weights, rows, grads in (
            (kept_ref, rows_ref, grad_ref), (other_ref, other_rows_ref, other_grad_ref)
        ):
            for kind, cols in enumerate((slice(0, two), slice(two, width))):
                picked = rows[kind * slots : (kind + 1) * slots, :].astype(F32)
                picked = picked.reshape(-1, local_experts, CAPACITY, depth)[:, e]
                picked = picked.reshape(count, depth).astype(BF)
                totals[kind] += jnp.dot(picked, weights[e, :, cols], preferred_element_type=F32)
                if kind == 1:
                    grads[e] = picked
        terms_ref[here, :two] = totals[0].astype(BF)
        terms_ref[here, two:] = totals[1].astype(BF)


def activate(terms_ref, out_ref):
    copies, rows, width = out_ref.shape
    width = width // 3

    def total(part):
        cols = slice(part * width, (part + 1) * width)
        return sum(terms_ref[i, :, cols].astype(F32) for i in range(terms_ref.shape[0]))

    gate, up_proj, d_hidden = total(0), total(1), total(2)
    sigmoid_gate = jax.nn.sigmoid(gate)
    silu_gate = gate * sigmoid_gate
    hidden = (silu_gate * up_proj).astype(BF)
    d_gate = (d_hidden * up_proj * sigmoid_gate * (1.0 + gate * (1.0 - sigmoid_gate))).astype(BF)
    d_up = (d_hidden * silu_gate).astype(BF)
    for i in range(copies):
        out_ref[i, :, :width] = hidden
        out_ref[i, :, width : 2 * width] = d_gate
        out_ref[i, :, 2 * width :] = d_up


def last_terms(member_ref, acts_ref, kept_ref, other_ref, parts_ref):
    local_experts, depth, width = kept_ref.shape
    one = width // 3
    count = acts_ref.shape[0] // local_experts
    half = depth // 2
    for weights, member in ((kept_ref, member_ref[0]), (other_ref, 1 - member_ref[0])):
        outs, grads = [], []
        for e in range(local_experts):
            here = slice(e * count, (e + 1) * count)
            out = lax.dot_general(
                acts_ref[here, :one], weights[e, :, 2 * one :], NT, preferred_element_type=F32
            )
            grad = lax.dot_general(
                acts_ref[here, one:], weights[e, :, : 2 * one], NT, preferred_element_type=F32
            )
            outs.append(out.reshape(count // CAPACITY, CAPACITY, depth))
            grads.append(grad.reshape(count // CAPACITY, CAPACITY, depth))
        out, grad = jnp.concatenate(outs, axis=1), jnp.concatenate(grads, axis=1)
        for j in range(2):
            cols = slice(j * half, (j + 1) * half)
            parts_ref[2 * j + member, :, :, :half] = out[:, :, cols].astype(BF)
            parts_ref[2 * j + member, :, :, half:] = grad[:, :, cols].astype(BF)


def down_terms(acts_ref, grad_ref, other_grad_ref, out_ref, other_out_ref):
    local_experts, count, _ = grad_ref.shape
    one = out_ref.shape[1]
    for e in range(local_experts):
        hidden = acts_ref[e * count : (e + 1) * count, :one]
        for grads, out in ((grad_ref, out_ref), (other_grad_ref, other_out_ref)):
            out[e] = lax.dot_general(hidden, grads[e], TN, preferred_element_type=F32).astype(BF)


def add_parts(parts_ref, out_ref):
    out_ref[...] = sum(parts_ref[i].astype(F32) for i in range(parts_ref.shape[0])).astype(BF)


def combine(slot_ref, weights_ref, back_ref, mixed_ref, grads_ref):
    top_count, tok_rows = slot_ref.shape
    slots, width = back_ref.shape[0] // 2, back_ref.shape[1]
    half = width // 2
    same = iota((tok_rows, tok_rows), 0) == iota((tok_rows, tok_rows), 1)

    def column(row):
        return jnp.sum(jnp.where(same, row, 0.0), axis=1, keepdims=True)

    mixed = jnp.zeros((tok_rows, half), F32)
    grads = jnp.zeros((tok_rows, half), F32)
    for k in range(top_count):
        slot = column(slot_ref[k : k + 1, :].astype(F32)).astype(jnp.int32)
        hot = jnp.where(iota((tok_rows, slots), 1) == slot, 1.0, 0.0).astype(BF)
        picked = jnp.dot(hot, back_ref[:slots, :], preferred_element_type=F32) + jnp.dot(
            hot, back_ref[slots:, :], preferred_element_type=F32
        )
        mixed = mixed + picked[:, :half] * column(weights_ref[k : k + 1, :])
        grads = grads + picked[:, half:]
    mixed_ref[...] = mixed.astype(BF)
    grads_ref[...] = grads.astype(BF)


def exchange(rows, axis):
    return lax.all_to_all(rows, axis, split_axis=0, concat_axis=0, tiled=True)


def swap(block):
    return lax.ppermute(block, "ym", [(0, 1), (1, 0)])


def shards(tokens, routes, route_weights, gate_weight, up_weight, down_weight, cotangent):
    local_experts, depth, width = gate_weight.shape
    groups = lax.axis_size("z") * lax.axis_size("xl")
    experts = groups * local_experts
    tok_rows, top_count = routes.shape
    slots = experts * CAPACITY
    count = groups * CAPACITY
    half = width // 2
    slices = lax.axis_size("yp") * lax.axis_size("xh")
    core = lax.axis_index("exp").reshape(1)
    member = lax.axis_index("ym").reshape(1)
    routes, route_weights = routes.T, route_weights.T

    weights = shape((local_experts, depth, 3 * half), BF)
    kept, given = call(
        pack, (weights, weights), member, gate_weight, up_weight, down_weight, scalars=1, given=3,
        scratch=[pltpu.VMEM(down_weight.shape, BF), pltpu.SemaphoreType.DMA((5,))],
    )
    send, slot_index = call(
        functools.partial(place_rows, experts),
        (shape((slots, depth), BF), shape((top_count, tok_rows), jnp.int32)),
        core, routes, route_weights, tokens, cotangent, scalars=1, given=4,
        scratch=[
            pltpu.VMEM(routes.shape, jnp.int32), pltpu.VMEM(routes.shape, F32),
            pltpu.VMEM(tokens.shape, BF), pltpu.VMEM(tokens.shape, BF),
            pltpu.SemaphoreType.DMA((4,)),
        ],
    )
    other = swap(given)
    arrived = exchange(send, ETP)
    other_arrived = swap(arrived)
    rows = lax.all_gather(arrived, "exp", axis=0, tiled=True)
    other_rows = lax.all_gather(other_arrived, "exp", axis=0, tiled=True)

    grads = shape((local_experts, count, depth), BF)
    terms, expert_grad, other_grad = call(
        first_terms, (shape((slots, 3 * half), BF), grads, grads), kept, other, rows, other_rows
    )
    terms = exchange(terms, ("yp", "xh")).reshape(slices, slots // slices, 3 * half)
    acts = call(activate, shape(terms.shape, BF), terms)
    acts = exchange(acts.reshape(slots, 3 * half), ("yp", "xh"))

    parts = call(
        last_terms, shape((4, groups, local_experts * CAPACITY, depth), BF),
        member, acts, kept, other, scalars=1,
    )
    parts = exchange(parts.reshape(4 * slots, depth), "exp").reshape(2, 2 * slots, depth)
    slot_sums = call(add_parts, shape((2 * slots, depth), BF), parts)
    back = exchange(slot_sums, ("ym",) + ETP)
    downs = shape((local_experts, half, depth), BF)
    d_down, other_down = call(down_terms, (downs, downs), acts, expert_grad, other_grad)
    other_down = swap(other_down)
    first = member[0] == 0
    d_down = jnp.concatenate(
        [jnp.where(first, d_down, other_down), jnp.where(first, other_down, d_down)], axis=1
    )
    mixed, d_tokens = call(
        combine,
        (shape((tok_rows, depth // 2), BF), shape((tok_rows, depth // 2), BF)),
        slot_index, route_weights, back,
    )
    return mixed, d_tokens, d_down


def solution(mesh):
    fine = Mesh(mesh.devices.reshape(4, 2, 2, 2, 8, 4), ("yp", "ym", "xh", "exp", "z", "xl"))
    dp = ("yp", "ym", "xh")
    in_specs = (
        P(ETP, dp),
        P(ETP, None),
        P(ETP, None),
        P(ETP, dp, "exp"),
        P(ETP, dp, "exp"),
        P(ETP, "exp", dp),
        P(ETP, dp),
    )
    out_specs = (P(ETP, dp + ("exp",)), P(ETP, dp + ("exp",)), P(ETP, "exp", dp))
    return jax.shard_map(shards, mesh=fine, in_specs=in_specs, out_specs=out_specs, check_vma=False)
```

```python
import functools

import jax
import jax.numpy as jnp
from jax import lax
from jax.experimental import pallas as pl
from jax.experimental.pallas import tpu as pltpu
from jax.sharding import Mesh, PartitionSpec as P

BF = jnp.bfloat16
F32 = jnp.float32
ETP = ("z", "xl")
CAPACITY = 8
VMEM = pl.BlockSpec(memory_space=pltpu.VMEM)
SMEM = pl.BlockSpec(memory_space=pltpu.SMEM)
HBM = pl.BlockSpec(memory_space=pltpu.HBM)
LIMIT = pltpu.CompilerParams(vmem_limit_bytes=40 * 1024 * 1024)
NT = (((1,), (1,)), ((), ()))
TN = (((0,), (0,)), ((), ()))


def call(kernel, outs, *args, scalars=0, given=0, scratch=()):
    rest = len(args) - scalars - given
    return pl.pallas_call(
        kernel,
        out_shape=outs,
        in_specs=[SMEM] * scalars + [HBM] * given + [VMEM] * rest,
        out_specs=jax.tree.map(lambda _: VMEM, outs),
        scratch_shapes=scratch,
        compiler_params=pltpu.CompilerParams(vmem_limit_bytes=(56 if given else 40) * 1024 * 1024),
    )(*args)


def shape(dims, kind):
    return jax.ShapeDtypeStruct(dims, kind)


def iota(dims, axis):
    return lax.broadcasted_iota(jnp.int32, dims, axis)


def pack(member_ref, gate_hbm, up_hbm, down_hbm, given_two, given_one, kept_ref, down, sems):
    local_experts, _, width = kept_ref.shape
    half = width // 3
    copies = [pltpu.make_async_copy(down_hbm, down, sems.at[0])]
    other = pl.ds(pl.multiple_of((1 - member_ref[0]) * half, 128), half)
    mine = pl.ds(pl.multiple_of(member_ref[0] * half, 128), half)
    for i, (out, units) in enumerate(((given_two, other), (kept_ref, mine))):
        for j, weights in enumerate((gate_hbm, up_hbm)):
            copies.append(
                pltpu.make_async_copy(
                    weights.at[:, :, units],
                    out.at[:, :, j * half : (j + 1) * half],
                    sems.at[1 + 2 * i + j],
                )
            )
    for copy in copies:
        copy.start()
    copies[0].wait()
    for e in range(local_experts):
        given_one[e] = down[e, other, :].T
        kept_ref[e, :, 2 * half :] = down[e, mine, :].T
    for copy in copies[1:]:
        copy.wait()


def place_rows(experts, core_ref, routes_hbm, weights_hbm, tokens_hbm, cot_hbm, packed, send_ref,
               slot_ref, routes_ref, weights_ref, tokens_ref, cot_ref, sems):
    copies = [
        pltpu.make_async_copy(source, target, sems.at[i])
        for i, (source, target) in enumerate(
            (
                (routes_hbm, routes_ref), (weights_hbm, weights_ref),
                (tokens_hbm, tokens_ref), (cot_hbm, cot_ref),
            )
        )
    ]
    for copy in copies:
        copy.start()
    for copy in copies[:2]:
        copy.wait()
    top_count, tok_rows = routes_ref.shape
    hots = [iota((experts, tok_rows), 0) == routes_ref[k : k + 1, :] for k in range(top_count)]
    both = sum(jnp.where(hot, 1.0, 0.0) for hot in hots)
    earlier = jnp.where(iota((tok_rows, tok_rows), 0) < iota((tok_rows, tok_rows), 1), 1.0, 0.0)
    count = jnp.dot(both.astype(BF), earlier.astype(BF), preferred_element_type=F32)
    placing = jnp.zeros((send_ref.shape[0], tok_rows), F32)
    slot_weight = jnp.zeros((send_ref.shape[0], 1), F32)
    for k, hot in enumerate(hots):
        position = jnp.sum(jnp.where(hot, count, 0.0), axis=0, keepdims=True).astype(jnp.int32)
        slot = routes_ref[k : k + 1, :] * CAPACITY + position
        slot_ref[k : k + 1, :] = slot
        hit = iota(placing.shape, 0) == slot
        placing = placing + jnp.where(hit, 1.0, 0.0)
        slot_weight = slot_weight + jnp.sum(
            jnp.where(hit, weights_ref[k : k + 1, :], 0.0), axis=1, keepdims=True
        )
    for copy in copies[2:]:
        copy.wait()
    first = core_ref[0] == 0
    source = jnp.where(first, tokens_ref[...].astype(F32), cot_ref[...].astype(F32)).astype(BF)
    scale = jnp.where(first, 1.0, slot_weight)
    rows = jnp.dot(placing.astype(BF), source, preferred_element_type=F32)
    send_ref[...] = (rows * scale).astype(BF)


def first_terms(kept_ref, two_ref, one_ref, rows_ref, other_rows_ref, terms_ref, grad_ref, other_grad_ref):
    local_experts, depth, width = kept_ref.shape
    two = width // 3 * 2
    slots = rows_ref.shape[0] // 2
    count = slots // local_experts

    def picked(rows, kind, e):
        taken = rows[kind * slots : (kind + 1) * slots, :].astype(F32)
        taken = taken.reshape(-1, local_experts, CAPACITY, depth)[:, e]
        return taken.reshape(count, depth).astype(BF)

    for e in range(local_experts):
        here = slice(e * count, (e + 1) * count)
        grad_ref[e], other_grad_ref[e] = picked(rows_ref, 1, e), picked(other_rows_ref, 1, e)
        terms_ref[here, :two] = (
            jnp.dot(picked(rows_ref, 0, e), kept_ref[e, :, :two], preferred_element_type=F32)
            + jnp.dot(picked(other_rows_ref, 0, e), two_ref[e], preferred_element_type=F32)
        ).astype(BF)
        terms_ref[here, two:] = (
            jnp.dot(grad_ref[e], kept_ref[e, :, two:], preferred_element_type=F32)
            + jnp.dot(other_grad_ref[e], one_ref[e], preferred_element_type=F32)
        ).astype(BF)


def activate(terms_ref, out_ref):
    copies, rows, width = out_ref.shape
    width = width // 3

    def total(part):
        cols = slice(part * width, (part + 1) * width)
        return sum(terms_ref[i, :, cols].astype(F32) for i in range(terms_ref.shape[0]))

    gate, up_proj, d_hidden = total(0), total(1), total(2)
    sigmoid_gate = jax.nn.sigmoid(gate)
    silu_gate = gate * sigmoid_gate
    hidden = (silu_gate * up_proj).astype(BF)
    d_gate = (d_hidden * up_proj * sigmoid_gate * (1.0 + gate * (1.0 - sigmoid_gate))).astype(BF)
    d_up = (d_hidden * silu_gate).astype(BF)
    for i in range(copies):
        out_ref[i, :, :width] = hidden
        out_ref[i, :, width : 2 * width] = d_gate
        out_ref[i, :, 2 * width :] = d_up


def last_terms(acts_ref, kept_ref, two_ref, one_ref, parts_ref):
    local_experts, depth, width = kept_ref.shape
    one = width // 3
    count = acts_ref.shape[0] // local_experts
    half = depth // 2

    def by_group(pieces):
        shaped = [p.reshape(count // CAPACITY, CAPACITY, depth) for p in pieces]
        return jnp.concatenate(shaped, axis=1)

    for side in range(2):
        outs, grads = [], []
        for e in range(local_experts):
            here = slice(e * count, (e + 1) * count)
            down = one_ref[e] if side else kept_ref[e, :, 2 * one :]
            two = two_ref[e] if side else kept_ref[e, :, : 2 * one]
            outs.append(
                lax.dot_general(acts_ref[here, :one], down, NT, preferred_element_type=F32)
            )
            grads.append(
                lax.dot_general(acts_ref[here, one:], two, NT, preferred_element_type=F32)
            )
        out, grad = by_group(outs), by_group(grads)
        for j in range(2):
            cols = slice(j * half, (j + 1) * half)
            parts_ref[2 * j + side, :, :, :half] = out[:, :, cols].astype(BF)
            parts_ref[2 * j + side, :, :, half:] = grad[:, :, cols].astype(BF)


def down_terms(acts_ref, grad_ref, other_grad_ref, out_ref, other_out_ref):
    local_experts, count, _ = grad_ref.shape
    one = out_ref.shape[1]
    for e in range(local_experts):
        hidden = acts_ref[e * count : (e + 1) * count, :one]
        for grads, out in ((grad_ref, out_ref), (other_grad_ref, other_out_ref)):
            out[e] = lax.dot_general(hidden, grads[e], TN, preferred_element_type=F32).astype(BF)


def add_parts(parts_ref, own_ref, out_ref, grad_ref):
    total = parts_ref[0].astype(F32) + parts_ref[1].astype(F32)
    slots, half = out_ref.shape
    own_ref[...] = total[:slots, :]
    out_ref[...] = total[slots:, :half].astype(BF)
    grad_ref[...] = total[slots:, half:].astype(BF)


def add_partners(own_ref, out_ref, grad_ref, sums_ref):
    half = out_ref.shape[1]
    sums_ref[:, :half] = (own_ref[:, :half] + out_ref[...].astype(F32)).astype(BF)
    sums_ref[:, half:] = (own_ref[:, half:] + grad_ref[...].astype(F32)).astype(BF)


def combine(slot_ref, weights_ref, back_ref, mixed_ref, grads_ref):
    top_count, tok_rows = slot_ref.shape
    slots, width = back_ref.shape
    half = width // 2
    same = iota((tok_rows, tok_rows), 0) == iota((tok_rows, tok_rows), 1)

    def column(row):
        return jnp.sum(jnp.where(same, row, 0.0), axis=1, keepdims=True)

    mixed = jnp.zeros((tok_rows, half), F32)
    grads = jnp.zeros((tok_rows, half), F32)
    for k in range(top_count):
        slot = column(slot_ref[k : k + 1, :].astype(F32)).astype(jnp.int32)
        hot = jnp.where(iota((tok_rows, slots), 1) == slot, 1.0, 0.0).astype(BF)
        picked = jnp.dot(hot, back_ref[...], preferred_element_type=F32)
        mixed = mixed + picked[:, :half] * column(weights_ref[k : k + 1, :])
        grads = grads + picked[:, half:]
    mixed_ref[...] = mixed.astype(BF)
    grads_ref[...] = grads.astype(BF)


def exchange(rows, axis):
    return lax.all_to_all(rows, axis, split_axis=0, concat_axis=0, tiled=True)


def neighbour(y, side):
    size = lax.axis_size("yp") * lax.axis_size("ym")
    return (y + (1 if y % 2 == side else -1)) % size


def swap(block, side):
    size = lax.axis_size("yp") * lax.axis_size("ym")
    return lax.ppermute(block, ("yp", "ym"), [(y, neighbour(y, side)) for y in range(size)])


def swap_rows(rows):
    size = lax.axis_size("yp") * lax.axis_size("ym")
    pairs = [(2 * y + c, 2 * neighbour(y, c) + c) for y in range(size) for c in range(2)]
    return lax.ppermute(rows, ("yp", "ym", "exp"), pairs)


def shards(tokens, routes, route_weights, gate_weight, up_weight, down_weight, cotangent):
    local_experts, depth, width = gate_weight.shape
    groups = lax.axis_size("z") * lax.axis_size("xl")
    experts = groups * local_experts
    tok_rows, top_count = routes.shape
    slots = experts * CAPACITY
    count = groups * CAPACITY
    half = width // 2
    slices = lax.axis_size("yp") * lax.axis_size("xh")
    core = lax.axis_index("exp").reshape(1)
    member = lax.axis_index("ym").reshape(1)
    routes, route_weights = routes.T, route_weights.T

    def weights(parts):
        return shape((local_experts, depth, parts * half), BF)

    given_two, given_one, kept = call(
        pack, (weights(2), weights(1), weights(3)), member, gate_weight, up_weight, down_weight,
        scalars=1, given=3,
        scratch=[pltpu.VMEM(down_weight.shape, BF), pltpu.SemaphoreType.DMA((5,))],
    )
    send, slot_index = call(
        functools.partial(place_rows, experts),
        (shape((slots, depth), BF), shape((top_count, tok_rows), jnp.int32)),
        core, routes, route_weights, tokens, cotangent, given_one, scalars=1, given=5,
        scratch=[
            pltpu.VMEM(routes.shape, jnp.int32), pltpu.VMEM(routes.shape, F32),
            pltpu.VMEM(tokens.shape, BF), pltpu.VMEM(tokens.shape, BF),
            pltpu.SemaphoreType.DMA((4,)),
        ],
    )
    two, one = swap(given_two, 0), swap(given_one, 1)
    arrived = exchange(send, ETP)
    arrived, two, one = lax.optimization_barrier((arrived, two, one))
    other_arrived = swap_rows(arrived)
    rows = lax.all_gather(arrived, "exp", axis=0, tiled=True)
    other_rows = lax.all_gather(other_arrived, "exp", axis=0, tiled=True)

    grads = shape((local_experts, count, depth), BF)
    terms, expert_grad, other_grad = call(
        first_terms, (shape((slots, 3 * half), BF), grads, grads), kept, two, one, rows, other_rows
    )
    terms = exchange(terms, ("yp", "xh")).reshape(slices, slots // slices, 3 * half)
    acts = call(activate, shape(terms.shape, BF), terms)
    acts = exchange(acts.reshape(slots, 3 * half), ("yp", "xh"))

    parts = call(
        last_terms, shape((4, groups, local_experts * CAPACITY, depth), BF), acts, kept, two, one
    )
    parts = exchange(parts.reshape(4 * slots, depth), "exp").reshape(2, 2 * slots, depth)
    part = shape((slots, depth // 2), BF)
    own, out_other, grad_other = call(add_parts, (shape((slots, depth), F32), part, part), parts)
    out_other, grad_other = swap(out_other, 1), swap(grad_other, 0)
    slot_sums = call(add_partners, shape((slots, depth), BF), own, out_other, grad_other)
    back = exchange(slot_sums, ETP)
    downs = shape((local_experts, half, depth), BF)
    d_down, other_down = call(down_terms, (downs, downs), acts, expert_grad, other_grad)
    other_down = swap(other_down, 1)
    first = member[0] == 0
    d_down = jnp.concatenate(
        [jnp.where(first, d_down, other_down), jnp.where(first, other_down, d_down)], axis=1
    )
    mixed, d_tokens = call(
        combine,
        (shape((tok_rows, depth // 2), BF), shape((tok_rows, depth // 2), BF)),
        slot_index, route_weights, back,
    )
    return mixed, d_tokens, d_down


def solution(mesh):
    fine = Mesh(mesh.devices.reshape(4, 2, 2, 2, 8, 4), ("yp", "ym", "xh", "exp", "z", "xl"))
    dp = ("yp", "ym", "xh")
    in_specs = (
        P(ETP, dp),
        P(ETP, None),
        P(ETP, None),
        P(ETP, dp, "exp"),
        P(ETP, dp, "exp"),
        P(ETP, "exp", dp),
        P(ETP, dp),
    )
    out_specs = (P(ETP, dp + ("exp",)), P(ETP, dp + ("exp",)), P(ETP, "exp", dp))
    return jax.shard_map(shards, mesh=fine, in_specs=in_specs, out_specs=out_specs, check_vma=False)
```

```python
import functools

import jax
import jax.numpy as jnp
from jax import lax
from jax.experimental import pallas as pl
from jax.experimental.pallas import tpu as pltpu
from jax.sharding import Mesh, PartitionSpec as P

BF = jnp.bfloat16
F32 = jnp.float32
ETP = ("z", "xl")
CAPACITY = 8
VMEM = pl.BlockSpec(memory_space=pltpu.VMEM)
SMEM = pl.BlockSpec(memory_space=pltpu.SMEM)
HBM = pl.BlockSpec(memory_space=pltpu.HBM)
LIMIT = pltpu.CompilerParams(vmem_limit_bytes=40 * 1024 * 1024)
NT = (((1,), (1,)), ((), ()))
TN = (((0,), (0,)), ((), ()))


def call(kernel, outs, *args, scalars=0, given=0, scratch=()):
    rest = len(args) - scalars - given
    return pl.pallas_call(
        kernel,
        out_shape=outs,
        in_specs=[SMEM] * scalars + [HBM] * given + [VMEM] * rest,
        out_specs=jax.tree.map(lambda _: VMEM, outs),
        scratch_shapes=scratch,
        compiler_params=pltpu.CompilerParams(vmem_limit_bytes=(56 if given else 40) * 1024 * 1024),
    )(*args)


def shape(dims, kind):
    return jax.ShapeDtypeStruct(dims, kind)


def iota(dims, axis):
    return lax.broadcasted_iota(jnp.int32, dims, axis)


def pack(member_ref, gate_hbm, up_hbm, down_hbm, kept_ref, given_ref, down, sems):
    local_experts, _, width = kept_ref.shape
    half = width // 3
    copies = [pltpu.make_async_copy(down_hbm, down, sems.at[0])]
    sides = ((given_ref, 1 - member_ref[0]), (kept_ref, member_ref[0]))
    for i, (out, member) in enumerate(sides):
        units = pl.ds(pl.multiple_of(member * half, 128), half)
        for j, weights in enumerate((gate_hbm, up_hbm)):
            copies.append(
                pltpu.make_async_copy(
                    weights.at[:, :, units],
                    out.at[:, :, j * half : (j + 1) * half],
                    sems.at[1 + 2 * i + j],
                )
            )
    for copy in copies:
        copy.start()
    copies[0].wait()
    for out, member in sides:
        units = pl.ds(pl.multiple_of(member * half, 128), half)
        for e in range(local_experts):
            out[e, :, 2 * half :] = down[e, units, :].T
    for copy in copies[1:]:
        copy.wait()


def place_rows(experts, core_ref, routes_hbm, weights_hbm, tokens_hbm, cot_hbm, send_ref, slot_ref,
               routes_ref, weights_ref, tokens_ref, cot_ref, sems):
    copies = [
        pltpu.make_async_copy(source, target, sems.at[i])
        for i, (source, target) in enumerate(
            (
                (routes_hbm, routes_ref), (weights_hbm, weights_ref),
                (tokens_hbm, tokens_ref), (cot_hbm, cot_ref),
            )
        )
    ]
    for copy in copies:
        copy.start()
    for copy in copies[:2]:
        copy.wait()
    top_count, tok_rows = routes_ref.shape
    hots = [iota((experts, tok_rows), 0) == routes_ref[k : k + 1, :] for k in range(top_count)]
    both = sum(jnp.where(hot, 1.0, 0.0) for hot in hots)
    earlier = jnp.where(iota((tok_rows, tok_rows), 0) < iota((tok_rows, tok_rows), 1), 1.0, 0.0)
    count = jnp.dot(both.astype(BF), earlier.astype(BF), preferred_element_type=F32)
    placing = jnp.zeros((send_ref.shape[0], tok_rows), F32)
    slot_weight = jnp.zeros((send_ref.shape[0], 1), F32)
    for k, hot in enumerate(hots):
        position = jnp.sum(jnp.where(hot, count, 0.0), axis=0, keepdims=True).astype(jnp.int32)
        slot = routes_ref[k : k + 1, :] * CAPACITY + position
        slot_ref[k : k + 1, :] = slot
        hit = iota(placing.shape, 0) == slot
        placing = placing + jnp.where(hit, 1.0, 0.0)
        slot_weight = slot_weight + jnp.sum(
            jnp.where(hit, weights_ref[k : k + 1, :], 0.0), axis=1, keepdims=True
        )
    for copy in copies[2:]:
        copy.wait()
    first = core_ref[0] == 0
    source = jnp.where(first, tokens_ref[...].astype(F32), cot_ref[...].astype(F32)).astype(BF)
    scale = jnp.where(first, 1.0, slot_weight)
    rows = jnp.dot(placing.astype(BF), source, preferred_element_type=F32)
    send_ref[...] = (rows * scale).astype(BF)


def first_terms(turn_ref, kept_ref, other_ref, rows_ref, other_rows_ref, *refs):
    own_ref, *messages, grad_ref, other_grad_ref, terms = refs
    local_experts, depth, width = kept_ref.shape
    two = width // 3 * 2
    slots = rows_ref.shape[0] // 2
    count = slots // local_experts
    for e in range(local_experts):
        here = slice(e * count, (e + 1) * count)
        totals = [0.0, 0.0]
        for weights, rows, grads in (
            (kept_ref, rows_ref, grad_ref), (other_ref, other_rows_ref, other_grad_ref)
        ):
            for kind, cols in enumerate((slice(0, two), slice(two, width))):
                picked = rows[kind * slots : (kind + 1) * slots, :].astype(F32)
                picked = picked.reshape(-1, local_experts, CAPACITY, depth)[:, e]
                picked = picked.reshape(count, depth).astype(BF)
                totals[kind] += jnp.dot(picked, weights[e, :, cols], preferred_element_type=F32)
                if kind == 1:
                    grads[e] = picked
        terms[here, :two] = totals[0]
        terms[here, two:] = totals[1]
    turns = 1 + len(messages)
    rows = own_ref.shape[0]
    for k, out in enumerate((own_ref, *messages)):
        base = pl.multiple_of(lax.rem(turn_ref[0] + k, turns) * rows, rows)
        out[...] = terms[pl.ds(base, rows), :].astype(out.dtype)


def add_terms(own_ref, *refs):
    *came, out_ref = refs
    out_ref[...] = (own_ref[...] + sum(piece[...].astype(F32) for piece in came)).astype(BF)


def activate(pair_ref, out_ref):
    rows, width = out_ref.shape[0], out_ref.shape[1] // 3

    def total(part):
        cols = slice(part * width, (part + 1) * width)
        return pair_ref[:rows, cols].astype(F32) + pair_ref[rows:, cols].astype(F32)

    gate, up_proj, d_hidden = total(0), total(1), total(2)
    sigmoid_gate = jax.nn.sigmoid(gate)
    silu_gate = gate * sigmoid_gate
    out_ref[:, :width] = (silu_gate * up_proj).astype(BF)
    out_ref[:, width : 2 * width] = (
        d_hidden * up_proj * sigmoid_gate * (1.0 + gate * (1.0 - sigmoid_gate))
    ).astype(BF)
    out_ref[:, 2 * width :] = (d_hidden * silu_gate).astype(BF)


def last_terms(member_ref, turn_ref, kept_ref, other_ref, *refs):
    *pieces, parts_ref, acts_ref = refs
    rows = pieces[0].shape[0]
    for k, piece in enumerate(pieces):
        turn = lax.rem(turn_ref[0] + (len(pieces) - k), len(pieces))
        acts_ref[pl.ds(pl.multiple_of(turn * rows, rows), rows), :] = piece[...]
    local_experts, depth, width = kept_ref.shape
    one = width // 3
    count = acts_ref.shape[0] // local_experts
    half = depth // 2
    for weights, member in ((kept_ref, member_ref[0]), (other_ref, 1 - member_ref[0])):
        outs, grads = [], []
        for e in range(local_experts):
            here = slice(e * count, (e + 1) * count)
            out = lax.dot_general(
                acts_ref[here, :one], weights[e, :, 2 * one :], NT, preferred_element_type=F32
            )
            grad = lax.dot_general(
                acts_ref[here, one:], weights[e, :, : 2 * one], NT, preferred_element_type=F32
            )
            outs.append(out.reshape(count // CAPACITY, CAPACITY, depth))
            grads.append(grad.reshape(count // CAPACITY, CAPACITY, depth))
        out, grad = jnp.concatenate(outs, axis=1), jnp.concatenate(grads, axis=1)
        for j in range(2):
            cols = slice(j * half, (j + 1) * half)
            parts_ref[2 * j + member, :, :, :half] = out[:, :, cols].astype(BF)
            parts_ref[2 * j + member, :, :, half:] = grad[:, :, cols].astype(BF)


def down_terms(acts_ref, grad_ref, other_grad_ref, out_ref, other_out_ref):
    local_experts, count, _ = grad_ref.shape
    one = out_ref.shape[1]
    for e in range(local_experts):
        hidden = acts_ref[e * count : (e + 1) * count, :one]
        for grads, out in ((grad_ref, out_ref), (other_grad_ref, other_out_ref)):
            out[e] = lax.dot_general(hidden, grads[e], TN, preferred_element_type=F32).astype(BF)


def add_parts(parts_ref, out_ref):
    out_ref[...] = sum(parts_ref[i].astype(F32) for i in range(parts_ref.shape[0])).astype(BF)


def combine(slot_ref, weights_ref, back_ref, mixed_ref, grads_ref):
    top_count, tok_rows = slot_ref.shape
    slots, width = back_ref.shape[0] // 2, back_ref.shape[1]
    half = width // 2
    same = iota((tok_rows, tok_rows), 0) == iota((tok_rows, tok_rows), 1)

    def column(row):
        return jnp.sum(jnp.where(same, row, 0.0), axis=1, keepdims=True)

    mixed = jnp.zeros((tok_rows, half), F32)
    grads = jnp.zeros((tok_rows, half), F32)
    for k in range(top_count):
        slot = column(slot_ref[k : k + 1, :].astype(F32)).astype(jnp.int32)
        hot = jnp.where(iota((tok_rows, slots), 1) == slot, 1.0, 0.0).astype(BF)
        picked = jnp.dot(hot, back_ref[:slots, :], preferred_element_type=F32) + jnp.dot(
            hot, back_ref[slots:, :], preferred_element_type=F32
        )
        mixed = mixed + picked[:, :half] * column(weights_ref[k : k + 1, :])
        grads = grads + picked[:, half:]
    mixed_ref[...] = mixed.astype(BF)
    grads_ref[...] = grads.astype(BF)


def exchange(rows, axis):
    return lax.all_to_all(rows, axis, split_axis=0, concat_axis=0, tiled=True)


def onward(block, turns):
    size = lax.axis_size("yp")
    return lax.ppermute(block, "yp", [(i, (i + turns) % size) for i in range(size)])


def swap(block):
    return lax.ppermute(block, "ym", [(0, 1), (1, 0)])


def shards(tokens, routes, route_weights, gate_weight, up_weight, down_weight, cotangent):
    local_experts, depth, width = gate_weight.shape
    groups = lax.axis_size("z") * lax.axis_size("xl")
    experts = groups * local_experts
    tok_rows, top_count = routes.shape
    slots = experts * CAPACITY
    count = groups * CAPACITY
    half = width // 2
    turns = lax.axis_size("yp")
    rows_each = slots // turns
    core = lax.axis_index("exp").reshape(1)
    member = lax.axis_index("ym").reshape(1)
    turn = lax.axis_index("yp").reshape(1)
    routes, route_weights = routes.T, route_weights.T

    weights = shape((local_experts, depth, 3 * half), BF)
    kept, given = call(
        pack, (weights, weights), member, gate_weight, up_weight, down_weight, scalars=1, given=3,
        scratch=[pltpu.VMEM(down_weight.shape, BF), pltpu.SemaphoreType.DMA((5,))],
    )
    send, slot_index = call(
        functools.partial(place_rows, experts),
        (shape((slots, depth), BF), shape((top_count, tok_rows), jnp.int32)),
        core, routes, route_weights, tokens, cotangent, scalars=1, given=4,
        scratch=[
            pltpu.VMEM(routes.shape, jnp.int32), pltpu.VMEM(routes.shape, F32),
            pltpu.VMEM(tokens.shape, BF), pltpu.VMEM(tokens.shape, BF),
            pltpu.SemaphoreType.DMA((4,)),
        ],
    )
    other = swap(given)
    arrived = exchange(send, ETP)
    other_arrived = swap(arrived)
    rows = lax.all_gather(arrived, "exp", axis=0, tiled=True)
    other_rows = lax.all_gather(other_arrived, "exp", axis=0, tiled=True)

    grads = shape((local_experts, count, depth), BF)
    block = shape((rows_each, 3 * half), BF)
    own, *messages, expert_grad, other_grad = call(
        first_terms,
        (shape(block.shape, F32),) + (block,) * (turns - 1) + (grads, grads),
        turn, kept, other, rows, other_rows, scalars=1,
        scratch=[pltpu.VMEM((slots, 3 * half), F32)],
    )
    came = [onward(message, k) for k, message in enumerate(messages, 1)]
    sums = call(add_terms, block, own, *came)
    acts = call(activate, block, lax.all_gather(sums, "xh", axis=0, tiled=True))
    pieces = [acts] + [onward(acts, k) for k in range(1, turns)]

    parts, acts = call(
        last_terms,
        (
            shape((4, groups, local_experts * CAPACITY, depth), BF),
            shape((slots, 3 * half), BF),
        ),
        member, turn, kept, other, *pieces, scalars=2,
    )
    parts = exchange(parts.reshape(4 * slots, depth), "exp").reshape(2, 2 * slots, depth)
    slot_sums = call(add_parts, shape((2 * slots, depth), BF), parts)
    back = exchange(slot_sums, ("ym",) + ETP)
    downs = shape((local_experts, half, depth), BF)
    d_down, other_down = call(down_terms, (downs, downs), acts, expert_grad, other_grad)
    other_down = swap(other_down)
    first = member[0] == 0
    d_down = jnp.concatenate(
        [jnp.where(first, d_down, other_down), jnp.where(first, other_down, d_down)], axis=1
    )
    mixed, d_tokens = call(
        combine,
        (shape((tok_rows, depth // 2), BF), shape((tok_rows, depth // 2), BF)),
        slot_index, route_weights, back,
    )
    return mixed, d_tokens, d_down


def solution(mesh):
    fine = Mesh(mesh.devices.reshape(4, 2, 2, 2, 8, 4), ("yp", "ym", "xh", "exp", "z", "xl"))
    dp = ("yp", "ym", "xh")
    in_specs = (
        P(ETP, dp),
        P(ETP, None),
        P(ETP, None),
        P(ETP, dp, "exp"),
        P(ETP, dp, "exp"),
        P(ETP, "exp", dp),
        P(ETP, dp),
    )
    out_specs = (P(ETP, dp + ("exp",)), P(ETP, dp + ("exp",)), P(ETP, "exp", dp))
    return jax.shard_map(shards, mesh=fine, in_specs=in_specs, out_specs=out_specs, check_vma=False)
```

```python
import functools

import jax
import jax.numpy as jnp
from jax import lax
from jax.experimental import pallas as pl
from jax.experimental.pallas import tpu as pltpu
from jax.sharding import Mesh, PartitionSpec as P

BF = jnp.bfloat16
F32 = jnp.float32
ETP = ("z", "xl")
CAPACITY = 8
VMEM = pl.BlockSpec(memory_space=pltpu.VMEM)
SMEM = pl.BlockSpec(memory_space=pltpu.SMEM)
HBM = pl.BlockSpec(memory_space=pltpu.HBM)
LIMIT = pltpu.CompilerParams(vmem_limit_bytes=40 * 1024 * 1024)
NT = (((1,), (1,)), ((), ()))
TN = (((0,), (0,)), ((), ()))


def call(kernel, outs, *args, scalars=0, given=0, scratch=()):
    rest = len(args) - scalars - given
    return pl.pallas_call(
        kernel,
        out_shape=outs,
        in_specs=[SMEM] * scalars + [HBM] * given + [VMEM] * rest,
        out_specs=jax.tree.map(lambda _: VMEM, outs),
        scratch_shapes=scratch,
        compiler_params=pltpu.CompilerParams(vmem_limit_bytes=(56 if given else 40) * 1024 * 1024),
    )(*args)


def shape(dims, kind):
    return jax.ShapeDtypeStruct(dims, kind)


def iota(dims, axis):
    return lax.broadcasted_iota(jnp.int32, dims, axis)


def begin(experts, core_ref, member_ref, routes_hbm, weights_hbm, tokens_hbm, cot_hbm, gate_hbm,
          up_hbm, down_hbm, send_ref, slot_ref, kept_ref, given_ref,
          routes_ref, weights_ref, tokens_ref, cot_ref, down, sems):
    local_experts, _, width = kept_ref.shape
    part = width // 3
    sides = [
        (out, pl.ds(pl.multiple_of(owner * part, 128), part))
        for out, owner in ((given_ref, 1 - member_ref[0]), (kept_ref, member_ref[0]))
    ]
    moves = [
        (routes_hbm, routes_ref), (weights_hbm, weights_ref), (down_hbm, down),
        (tokens_hbm, tokens_ref), (cot_hbm, cot_ref),
    ]
    for out, units in sides:
        for j, source in enumerate((gate_hbm, up_hbm)):
            target = out.at[:, :, j * part : (j + 1) * part]
            moves.append((source.at[:, :, units], target))
    copies = [pltpu.make_async_copy(a, b, sems.at[i]) for i, (a, b) in enumerate(moves)]
    for copy in copies:
        copy.start()
    for copy in copies[:3]:
        copy.wait()
    for out, units in sides:
        for e in range(local_experts):
            out[e, :, 2 * part :] = down[e, units, :].T
    top_count, tok_rows = routes_ref.shape
    hots = [iota((experts, tok_rows), 0) == routes_ref[k : k + 1, :] for k in range(top_count)]
    both = sum(jnp.where(hot, 1.0, 0.0) for hot in hots)
    earlier = jnp.where(iota((tok_rows, tok_rows), 0) < iota((tok_rows, tok_rows), 1), 1.0, 0.0)
    count = jnp.dot(both.astype(BF), earlier.astype(BF), preferred_element_type=F32)
    placing = jnp.zeros((send_ref.shape[0], tok_rows), F32)
    slot_weight = jnp.zeros((send_ref.shape[0], 1), F32)
    for k, hot in enumerate(hots):
        position = jnp.sum(jnp.where(hot, count, 0.0), axis=0, keepdims=True).astype(jnp.int32)
        slot = routes_ref[k : k + 1, :] * CAPACITY + position
        slot_ref[k : k + 1, :] = slot
        hit = iota(placing.shape, 0) == slot
        placing = placing + jnp.where(hit, 1.0, 0.0)
        slot_weight = slot_weight + jnp.sum(
            jnp.where(hit, weights_ref[k : k + 1, :], 0.0), axis=1, keepdims=True
        )
    for copy in copies[3:]:
        copy.wait()
    first = core_ref[0] == 0
    source = jnp.where(first, tokens_ref[...].astype(F32), cot_ref[...].astype(F32)).astype(BF)
    scale = jnp.where(first, 1.0, slot_weight)
    rows = jnp.dot(placing.astype(BF), source, preferred_element_type=F32)
    send_ref[...] = (rows * scale).astype(BF)


def first_terms(kept_ref, other_ref, rows_ref, other_rows_ref, terms_ref, grad_ref, other_grad_ref):
    local_experts, depth, width = kept_ref.shape
    two = width // 3 * 2
    slots = rows_ref.shape[0] // 2
    count = slots // local_experts
    for e in range(local_experts):
        here = slice(e * count, (e + 1) * count)
        totals = [0.0, 0.0]
        for weights, rows, grads in (
            (kept_ref, rows_ref, grad_ref), (other_ref, other_rows_ref, other_grad_ref)
        ):
            for kind, cols in enumerate((slice(0, two), slice(two, width))):
                picked = rows[kind * slots : (kind + 1) * slots, :].astype(F32)
                picked = picked.reshape(-1, local_experts, CAPACITY, depth)[:, e]
                picked = picked.reshape(count, depth).astype(BF)
                totals[kind] += jnp.dot(picked, weights[e, :, cols], preferred_element_type=F32)
                if kind == 1:
                    grads[e] = picked
        terms_ref[here, :two] = totals[0].astype(BF)
        terms_ref[here, two:] = totals[1].astype(BF)


def activate(terms_ref, out_ref):
    copies, rows, width = out_ref.shape
    width = width // 3

    def total(part):
        cols = slice(part * width, (part + 1) * width)
        return sum(terms_ref[i, :, cols].astype(F32) for i in range(terms_ref.shape[0]))

    gate, up_proj, d_hidden = total(0), total(1), total(2)
    sigmoid_gate = jax.nn.sigmoid(gate)
    silu_gate = gate * sigmoid_gate
    hidden = (silu_gate * up_proj).astype(BF)
    d_gate = (d_hidden * up_proj * sigmoid_gate * (1.0 + gate * (1.0 - sigmoid_gate))).astype(BF)
    d_up = (d_hidden * silu_gate).astype(BF)
    for i in range(copies):
        out_ref[i, :, :width] = hidden
        out_ref[i, :, width : 2 * width] = d_gate
        out_ref[i, :, 2 * width :] = d_up


def last_terms(member_ref, acts_ref, kept_ref, other_ref, parts_ref):
    local_experts, depth, width = kept_ref.shape
    one = width // 3
    count = acts_ref.shape[0] // local_experts
    half = depth // 2
    for weights, member in ((kept_ref, member_ref[0]), (other_ref, 1 - member_ref[0])):
        outs, grads = [], []
        for e in range(local_experts):
            here = slice(e * count, (e + 1) * count)
            out = lax.dot_general(
                acts_ref[here, :one], weights[e, :, 2 * one :], NT, preferred_element_type=F32
            )
            grad = lax.dot_general(
                acts_ref[here, one:], weights[e, :, : 2 * one], NT, preferred_element_type=F32
            )
            outs.append(out.reshape(count // CAPACITY, CAPACITY, depth))
            grads.append(grad.reshape(count // CAPACITY, CAPACITY, depth))
        out, grad = jnp.concatenate(outs, axis=1), jnp.concatenate(grads, axis=1)
        for j in range(2):
            cols = slice(j * half, (j + 1) * half)
            parts_ref[2 * j + member, :, :, :half] = out[:, :, cols].astype(BF)
            parts_ref[2 * j + member, :, :, half:] = grad[:, :, cols].astype(BF)


def down_terms(acts_ref, grad_ref, other_grad_ref, out_ref, other_out_ref):
    local_experts, count, _ = grad_ref.shape
    one = out_ref.shape[1]
    for e in range(local_experts):
        hidden = acts_ref[e * count : (e + 1) * count, :one]
        for grads, out in ((grad_ref, out_ref), (other_grad_ref, other_out_ref)):
            out[e] = lax.dot_general(hidden, grads[e], TN, preferred_element_type=F32).astype(BF)


def add_parts(parts_ref, out_ref):
    out_ref[...] = sum(parts_ref[i].astype(F32) for i in range(parts_ref.shape[0])).astype(BF)


def combine(slot_ref, weights_ref, back_ref, mixed_ref, grads_ref):
    top_count, tok_rows = slot_ref.shape
    slots, width = back_ref.shape[0] // 2, back_ref.shape[1]
    half = width // 2
    same = iota((tok_rows, tok_rows), 0) == iota((tok_rows, tok_rows), 1)

    def column(row):
        return jnp.sum(jnp.where(same, row, 0.0), axis=1, keepdims=True)

    mixed = jnp.zeros((tok_rows, half), F32)
    grads = jnp.zeros((tok_rows, half), F32)
    for k in range(top_count):
        slot = column(slot_ref[k : k + 1, :].astype(F32)).astype(jnp.int32)
        hot = jnp.where(iota((tok_rows, slots), 1) == slot, 1.0, 0.0).astype(BF)
        picked = jnp.dot(hot, back_ref[:slots, :], preferred_element_type=F32) + jnp.dot(
            hot, back_ref[slots:, :], preferred_element_type=F32
        )
        mixed = mixed + picked[:, :half] * column(weights_ref[k : k + 1, :])
        grads = grads + picked[:, half:]
    mixed_ref[...] = mixed.astype(BF)
    grads_ref[...] = grads.astype(BF)


def exchange(rows, axis):
    return lax.all_to_all(rows, axis, split_axis=0, concat_axis=0, tiled=True)


def swap(block):
    return lax.ppermute(block, "ym", [(0, 1), (1, 0)])


def shards(tokens, routes, route_weights, gate_weight, up_weight, down_weight, cotangent):
    local_experts, depth, width = gate_weight.shape
    groups = lax.axis_size("z") * lax.axis_size("xl")
    experts = groups * local_experts
    tok_rows, top_count = routes.shape
    slots = experts * CAPACITY
    count = groups * CAPACITY
    half = width // 2
    slices = lax.axis_size("yp") * lax.axis_size("xh")
    core = lax.axis_index("exp").reshape(1)
    member = lax.axis_index("ym").reshape(1)
    routes, route_weights = routes.T, route_weights.T

    weights = shape((local_experts, depth, 3 * half), BF)
    send, slot_index, kept, given = call(
        functools.partial(begin, experts),
        (shape((slots, depth), BF), shape((top_count, tok_rows), jnp.int32), weights, weights),
        core, member, routes, route_weights, tokens, cotangent, gate_weight, up_weight,
        down_weight, scalars=2, given=7,
        scratch=[
            pltpu.VMEM(routes.shape, jnp.int32), pltpu.VMEM(routes.shape, F32),
            pltpu.VMEM(tokens.shape, BF), pltpu.VMEM(tokens.shape, BF),
            pltpu.VMEM(down_weight.shape, BF), pltpu.SemaphoreType.DMA((9,)),
        ],
    )
    other = swap(given)
    arrived = exchange(send, ETP)
    other_arrived = swap(arrived)
    rows = lax.all_gather(arrived, "exp", axis=0, tiled=True)
    other_rows = lax.all_gather(other_arrived, "exp", axis=0, tiled=True)

    grads = shape((local_experts, count, depth), BF)
    terms, expert_grad, other_grad = call(
        first_terms, (shape((slots, 3 * half), BF), grads, grads), kept, other, rows, other_rows
    )
    terms = exchange(terms, ("yp", "xh")).reshape(slices, slots // slices, 3 * half)
    acts = call(activate, shape(terms.shape, BF), terms)
    acts = exchange(acts.reshape(slots, 3 * half), ("yp", "xh"))

    parts = call(
        last_terms, shape((4, groups, local_experts * CAPACITY, depth), BF),
        member, acts, kept, other, scalars=1,
    )
    parts = exchange(parts.reshape(4 * slots, depth), "exp").reshape(2, 2 * slots, depth)
    slot_sums = call(add_parts, shape((2 * slots, depth), BF), parts)
    back = exchange(slot_sums, ("ym",) + ETP)
    downs = shape((local_experts, half, depth), BF)
    d_down, other_down = call(down_terms, (downs, downs), acts, expert_grad, other_grad)
    other_down = swap(other_down)
    first = member[0] == 0
    d_down = jnp.concatenate(
        [jnp.where(first, d_down, other_down), jnp.where(first, other_down, d_down)], axis=1
    )
    mixed, d_tokens = call(
        combine,
        (shape((tok_rows, depth // 2), BF), shape((tok_rows, depth // 2), BF)),
        slot_index, route_weights, back,
    )
    return mixed, d_tokens, d_down


def solution(mesh):
    fine = Mesh(mesh.devices.reshape(4, 2, 2, 2, 8, 4), ("yp", "ym", "xh", "exp", "z", "xl"))
    dp = ("yp", "ym", "xh")
    in_specs = (
        P(ETP, dp),
        P(ETP, None),
        P(ETP, None),
        P(ETP, dp, "exp"),
        P(ETP, dp, "exp"),
        P(ETP, "exp", dp),
        P(ETP, dp),
    )
    out_specs = (P(ETP, dp + ("exp",)), P(ETP, dp + ("exp",)), P(ETP, "exp", dp))
    return jax.shard_map(shards, mesh=fine, in_specs=in_specs, out_specs=out_specs, check_vma=False)
```

```python
import functools

import jax
import jax.numpy as jnp
from jax import lax
from jax.experimental import pallas as pl
from jax.experimental.pallas import tpu as pltpu
from jax.sharding import Mesh, PartitionSpec as P

BF = jnp.bfloat16
F32 = jnp.float32
ETP = ("z", "xl")
CAPACITY = 8
VMEM = pl.BlockSpec(memory_space=pltpu.VMEM)
SMEM = pl.BlockSpec(memory_space=pltpu.SMEM)
HBM = pl.BlockSpec(memory_space=pltpu.HBM)
LIMIT = pltpu.CompilerParams(vmem_limit_bytes=40 * 1024 * 1024)
NT = (((1,), (1,)), ((), ()))
TN = (((0,), (0,)), ((), ()))


def call(kernel, outs, *args, scalars=0, given=0, scratch=(), cost=None):
    rest = len(args) - scalars - given
    return pl.pallas_call(
        kernel,
        out_shape=outs,
        in_specs=[SMEM] * scalars + [HBM] * given + [VMEM] * rest,
        out_specs=jax.tree.map(lambda _: VMEM, outs),
        scratch_shapes=scratch,
        cost_estimate=cost,
        compiler_params=pltpu.CompilerParams(vmem_limit_bytes=(56 if given else 40) * 1024 * 1024),
    )(*args)


def shape(dims, kind):
    return jax.ShapeDtypeStruct(dims, kind)


def iota(dims, axis):
    return lax.broadcasted_iota(jnp.int32, dims, axis)


def begin(experts, core_ref, member_ref, routes_hbm, weights_hbm, tokens_hbm, cot_hbm, gate_hbm,
          up_hbm, down_hbm, send_ref, slot_ref, kept_ref, given_ref,
          routes_ref, weights_ref, tokens_ref, cot_ref, down, sems):
    local_experts, _, width = kept_ref.shape
    part = width // 3
    sides = [
        (out, pl.ds(pl.multiple_of(owner * part, 128), part))
        for out, owner in ((given_ref, 1 - member_ref[0]), (kept_ref, member_ref[0]))
    ]
    moves = [
        (routes_hbm, routes_ref), (weights_hbm, weights_ref), (down_hbm, down),
        (tokens_hbm, tokens_ref), (cot_hbm, cot_ref),
    ]
    for out, units in sides:
        for j, source in enumerate((gate_hbm, up_hbm)):
            target = out.at[:, :, j * part : (j + 1) * part]
            moves.append((source.at[:, :, units], target))
    copies = [pltpu.make_async_copy(a, b, sems.at[i]) for i, (a, b) in enumerate(moves)]
    for copy in copies:
        copy.start()
    for copy in copies[:3]:
        copy.wait()
    for out, units in sides:
        for e in range(local_experts):
            out[e, :, 2 * part :] = down[e, units, :].T
    top_count, tok_rows = routes_ref.shape
    hots = [iota((experts, tok_rows), 0) == routes_ref[k : k + 1, :] for k in range(top_count)]
    both = sum(jnp.where(hot, 1.0, 0.0) for hot in hots)
    earlier = jnp.where(iota((tok_rows, tok_rows), 0) < iota((tok_rows, tok_rows), 1), 1.0, 0.0)
    count = jnp.dot(both.astype(BF), earlier.astype(BF), preferred_element_type=F32)
    placing = jnp.zeros((send_ref.shape[0], tok_rows), F32)
    slot_weight = jnp.zeros((send_ref.shape[0], 1), F32)
    for k, hot in enumerate(hots):
        position = jnp.sum(jnp.where(hot, count, 0.0), axis=0, keepdims=True).astype(jnp.int32)
        slot = routes_ref[k : k + 1, :] * CAPACITY + position
        slot_ref[k : k + 1, :] = slot
        hit = iota(placing.shape, 0) == slot
        placing = placing + jnp.where(hit, 1.0, 0.0)
        slot_weight = slot_weight + jnp.sum(
            jnp.where(hit, weights_ref[k : k + 1, :], 0.0), axis=1, keepdims=True
        )
    for copy in copies[3:]:
        copy.wait()
    first = core_ref[0] == 0
    source = jnp.where(first, tokens_ref[...].astype(F32), cot_ref[...].astype(F32)).astype(BF)
    scale = jnp.where(first, 1.0, slot_weight)
    rows = jnp.dot(placing.astype(BF), source, preferred_element_type=F32)
    send_ref[...] = (rows * scale).astype(BF)


def first_terms(kept_ref, other_ref, rows_ref, other_rows_ref, terms_ref, grad_ref, other_grad_ref):
    local_experts, depth, width = kept_ref.shape
    two = width // 3 * 2
    slots = rows_ref.shape[0] // 2
    count = slots // local_experts
    for e in range(local_experts):
        here = slice(e * count, (e + 1) * count)
        totals = [0.0, 0.0]
        for weights, rows, grads in (
            (kept_ref, rows_ref, grad_ref), (other_ref, other_rows_ref, other_grad_ref)
        ):
            for kind, cols in enumerate((slice(0, two), slice(two, width))):
                picked = rows[kind * slots : (kind + 1) * slots, :].astype(F32)
                picked = picked.reshape(-1, local_experts, CAPACITY, depth)[:, e]
                picked = picked.reshape(count, depth).astype(BF)
                totals[kind] += jnp.dot(picked, weights[e, :, cols], preferred_element_type=F32)
                if kind == 1:
                    grads[e] = picked
        terms_ref[here, :two] = totals[0].astype(BF)
        terms_ref[here, two:] = totals[1].astype(BF)


def activate(terms_ref, out_ref):
    copies, rows, width = out_ref.shape
    width = width // 3

    def total(part):
        cols = slice(part * width, (part + 1) * width)
        return sum(terms_ref[i, :, cols].astype(F32) for i in range(terms_ref.shape[0]))

    gate, up_proj, d_hidden = total(0), total(1), total(2)
    sigmoid_gate = jax.nn.sigmoid(gate)
    silu_gate = gate * sigmoid_gate
    hidden = (silu_gate * up_proj).astype(BF)
    d_gate = (d_hidden * up_proj * sigmoid_gate * (1.0 + gate * (1.0 - sigmoid_gate))).astype(BF)
    d_up = (d_hidden * silu_gate).astype(BF)
    for i in range(copies):
        out_ref[i, :, :width] = hidden
        out_ref[i, :, width : 2 * width] = d_gate
        out_ref[i, :, 2 * width :] = d_up


def last_terms(member_ref, acts_ref, kept_ref, other_ref, parts_ref):
    local_experts, depth, width = kept_ref.shape
    one = width // 3
    count = acts_ref.shape[0] // local_experts
    half = depth // 2
    for weights, member in ((kept_ref, member_ref[0]), (other_ref, 1 - member_ref[0])):
        outs, grads = [], []
        for e in range(local_experts):
            here = slice(e * count, (e + 1) * count)
            out = lax.dot_general(
                acts_ref[here, :one], weights[e, :, 2 * one :], NT, preferred_element_type=F32
            )
            grad = lax.dot_general(
                acts_ref[here, one:], weights[e, :, : 2 * one], NT, preferred_element_type=F32
            )
            outs.append(out.reshape(count // CAPACITY, CAPACITY, depth))
            grads.append(grad.reshape(count // CAPACITY, CAPACITY, depth))
        out, grad = jnp.concatenate(outs, axis=1), jnp.concatenate(grads, axis=1)
        for j in range(2):
            cols = slice(j * half, (j + 1) * half)
            parts_ref[2 * j + member, :, :, :half] = out[:, :, cols].astype(BF)
            parts_ref[2 * j + member, :, :, half:] = grad[:, :, cols].astype(BF)


def down_terms(acts_ref, grad_ref, other_grad_ref, out_ref, other_out_ref):
    local_experts, count, _ = grad_ref.shape
    one = out_ref.shape[1]
    for e in range(local_experts):
        hidden = acts_ref[e * count : (e + 1) * count, :one]
        for grads, out in ((grad_ref, out_ref), (other_grad_ref, other_out_ref)):
            out[e] = lax.dot_general(hidden, grads[e], TN, preferred_element_type=F32).astype(BF)


def join(member_ref, mine_ref, other_ref, out_ref):
    half = mine_ref.shape[1]
    for source, member in ((mine_ref, member_ref[0]), (other_ref, 1 - member_ref[0])):
        units = pl.ds(pl.multiple_of(member * half, half), half)
        out_ref[:, units, :] = source[...]


def add_parts(parts_ref, out_ref):
    out_ref[...] = sum(parts_ref[i].astype(F32) for i in range(parts_ref.shape[0])).astype(BF)


def combine(slot_ref, weights_ref, back_ref, mixed_ref, grads_ref):
    top_count, tok_rows = slot_ref.shape
    slots, width = back_ref.shape[0] // 2, back_ref.shape[1]
    half = width // 2
    same = iota((tok_rows, tok_rows), 0) == iota((tok_rows, tok_rows), 1)

    def column(row):
        return jnp.sum(jnp.where(same, row, 0.0), axis=1, keepdims=True)

    mixed = jnp.zeros((tok_rows, half), F32)
    grads = jnp.zeros((tok_rows, half), F32)
    for k in range(top_count):
        slot = column(slot_ref[k : k + 1, :].astype(F32)).astype(jnp.int32)
        hot = jnp.where(iota((tok_rows, slots), 1) == slot, 1.0, 0.0).astype(BF)
        picked = jnp.dot(hot, back_ref[:slots, :], preferred_element_type=F32) + jnp.dot(
            hot, back_ref[slots:, :], preferred_element_type=F32
        )
        mixed = mixed + picked[:, :half] * column(weights_ref[k : k + 1, :])
        grads = grads + picked[:, half:]
    mixed_ref[...] = mixed.astype(BF)
    grads_ref[...] = grads.astype(BF)


def exchange(rows, axis):
    return lax.all_to_all(rows, axis, split_axis=0, concat_axis=0, tiled=True)


def swap(block):
    return lax.ppermute(block, "ym", [(0, 1), (1, 0)])


def shards(tokens, routes, route_weights, gate_weight, up_weight, down_weight, cotangent):
    local_experts, depth, width = gate_weight.shape
    groups = lax.axis_size("z") * lax.axis_size("xl")
    experts = groups * local_experts
    tok_rows, top_count = routes.shape
    slots = experts * CAPACITY
    count = groups * CAPACITY
    half = width // 2
    slices = lax.axis_size("yp") * lax.axis_size("xh")
    core = lax.axis_index("exp").reshape(1)
    member = lax.axis_index("ym").reshape(1)
    routes, route_weights = routes.T, route_weights.T

    weights = shape((local_experts, depth, 3 * half), BF)
    send, slot_index, kept, given = call(
        functools.partial(begin, experts),
        (shape((slots, depth), BF), shape((top_count, tok_rows), jnp.int32), weights, weights),
        core, member, routes, route_weights, tokens, cotangent, gate_weight, up_weight,
        down_weight, scalars=2, given=7,
        scratch=[
            pltpu.VMEM(routes.shape, jnp.int32), pltpu.VMEM(routes.shape, F32),
            pltpu.VMEM(tokens.shape, BF), pltpu.VMEM(tokens.shape, BF),
            pltpu.VMEM(down_weight.shape, BF), pltpu.SemaphoreType.DMA((9,)),
        ],
    )
    other = swap(given)
    arrived = exchange(send, ETP)
    other_arrived = swap(arrived)
    rows = lax.all_gather(arrived, "exp", axis=0, tiled=True)
    other_rows = lax.all_gather(other_arrived, "exp", axis=0, tiled=True)

    grads = shape((local_experts, count, depth), BF)
    terms, expert_grad, other_grad = call(
        first_terms, (shape((slots, 3 * half), BF), grads, grads), kept, other, rows, other_rows
    )
    terms = exchange(terms, ("yp", "xh")).reshape(slices, slots // slices, 3 * half)
    acts = call(activate, shape(terms.shape, BF), terms)
    acts = exchange(acts.reshape(slots, 3 * half), ("yp", "xh"))

    parts = call(
        last_terms, shape((4, groups, local_experts * CAPACITY, depth), BF),
        member, acts, kept, other, scalars=1,
    )
    parts = exchange(parts.reshape(4 * slots, depth), "exp").reshape(2, 2 * slots, depth)
    slot_sums = call(add_parts, shape((2 * slots, depth), BF), parts)
    back = exchange(slot_sums, ("ym",) + ETP)
    downs = shape((local_experts, half, depth), BF)
    d_down, other_down = call(down_terms, (downs, downs), acts, expert_grad, other_grad)
    other_down = swap(other_down)
    d_down = call(
        join, shape(down_weight.shape, BF), member, d_down, other_down, scalars=1,
        cost=pl.CostEstimate(flops=30_000_000_000, bytes_accessed=1 << 20, transcendentals=0),
    )
    mixed, d_tokens = call(
        combine,
        (shape((tok_rows, depth // 2), BF), shape((tok_rows, depth // 2), BF)),
        slot_index, route_weights, back,
    )
    return mixed, d_tokens, d_down


def solution(mesh):
    fine = Mesh(mesh.devices.reshape(4, 2, 2, 2, 8, 4), ("yp", "ym", "xh", "exp", "z", "xl"))
    dp = ("yp", "ym", "xh")
    in_specs = (
        P(ETP, dp),
        P(ETP, None),
        P(ETP, None),
        P(ETP, dp, "exp"),
        P(ETP, dp, "exp"),
        P(ETP, "exp", dp),
        P(ETP, dp),
    )
    out_specs = (P(ETP, dp + ("exp",)), P(ETP, dp + ("exp",)), P(ETP, "exp", dp))
    return jax.shard_map(shards, mesh=fine, in_specs=in_specs, out_specs=out_specs, check_vma=False)
```

```python
import functools

import jax
import jax.numpy as jnp
from jax import lax
from jax.experimental import pallas as pl
from jax.experimental.pallas import tpu as pltpu
from jax.sharding import Mesh, PartitionSpec as P

BF = jnp.bfloat16
F32 = jnp.float32
ETP = ("z", "xl")
CAPACITY = 8
VMEM = pl.BlockSpec(memory_space=pltpu.VMEM)
SMEM = pl.BlockSpec(memory_space=pltpu.SMEM)
HBM = pl.BlockSpec(memory_space=pltpu.HBM)
LIMIT = pltpu.CompilerParams(vmem_limit_bytes=40 * 1024 * 1024)
NT = (((1,), (1,)), ((), ()))
TN = (((0,), (0,)), ((), ()))


def call(kernel, outs, *args, scalars=0, given=0, scratch=()):
    rest = len(args) - scalars - given
    return pl.pallas_call(
        kernel,
        out_shape=outs,
        in_specs=[SMEM] * scalars + [HBM] * given + [VMEM] * rest,
        out_specs=jax.tree.map(lambda _: VMEM, outs),
        scratch_shapes=scratch,
        compiler_params=pltpu.CompilerParams(vmem_limit_bytes=(56 if given else 40) * 1024 * 1024),
    )(*args)


def shape(dims, kind):
    return jax.ShapeDtypeStruct(dims, kind)


def iota(dims, axis):
    return lax.broadcasted_iota(jnp.int32, dims, axis)


def begin(experts, core_ref, member_ref, routes_hbm, weights_hbm, tokens_hbm, cot_hbm, gate_hbm,
          up_hbm, down_hbm, send_ref, slot_ref, kept_ref, given_ref,
          routes_ref, weights_ref, tokens_ref, cot_ref, down, sems):
    local_experts, _, width = kept_ref.shape
    part = width // 3
    sides = [
        (out, pl.ds(pl.multiple_of(owner * part, 128), part))
        for out, owner in ((given_ref, 1 - member_ref[0]), (kept_ref, member_ref[0]))
    ]
    moves = [
        (routes_hbm, routes_ref), (weights_hbm, weights_ref), (down_hbm, down),
        (tokens_hbm, tokens_ref), (cot_hbm, cot_ref),
    ]
    for out, units in sides:
        for j, source in enumerate((gate_hbm, up_hbm)):
            target = out.at[:, :, j * part : (j + 1) * part]
            moves.append((source.at[:, :, units], target))
    copies = [pltpu.make_async_copy(a, b, sems.at[i]) for i, (a, b) in enumerate(moves)]
    for copy in copies:
        copy.start()
    for copy in copies[:3]:
        copy.wait()
    for out, units in sides:
        for e in range(local_experts):
            out[e, :, 2 * part :] = down[e, units, :].T
    top_count, tok_rows = routes_ref.shape
    hots = [iota((experts, tok_rows), 0) == routes_ref[k : k + 1, :] for k in range(top_count)]
    both = sum(jnp.where(hot, 1.0, 0.0) for hot in hots)
    earlier = jnp.where(iota((tok_rows, tok_rows), 0) < iota((tok_rows, tok_rows), 1), 1.0, 0.0)
    count = jnp.dot(both.astype(BF), earlier.astype(BF), preferred_element_type=F32)
    placing = jnp.zeros((send_ref.shape[0], tok_rows), F32)
    slot_weight = jnp.zeros((send_ref.shape[0], 1), F32)
    for k, hot in enumerate(hots):
        position = jnp.sum(jnp.where(hot, count, 0.0), axis=0, keepdims=True).astype(jnp.int32)
        slot = routes_ref[k : k + 1, :] * CAPACITY + position
        slot_ref[k : k + 1, :] = slot
        hit = iota(placing.shape, 0) == slot
        placing = placing + jnp.where(hit, 1.0, 0.0)
        slot_weight = slot_weight + jnp.sum(
            jnp.where(hit, weights_ref[k : k + 1, :], 0.0), axis=1, keepdims=True
        )
    for copy in copies[3:]:
        copy.wait()
    first = core_ref[0] == 0
    source = jnp.where(first, tokens_ref[...].astype(F32), cot_ref[...].astype(F32)).astype(BF)
    scale = jnp.where(first, 1.0, slot_weight)
    rows = jnp.dot(placing.astype(BF), source, preferred_element_type=F32)
    send_ref[...] = (rows * scale).astype(BF)


def first_terms(kept_ref, other_ref, rows_ref, other_rows_ref, terms_ref, grad_ref, other_grad_ref):
    local_experts, depth, width = kept_ref.shape
    two = width // 3 * 2
    slots = rows_ref.shape[0] // 2
    count = slots // local_experts
    for e in range(local_experts):
        here = slice(e * count, (e + 1) * count)
        totals = [0.0, 0.0]
        for weights, rows, grads in (
            (kept_ref, rows_ref, grad_ref), (other_ref, other_rows_ref, other_grad_ref)
        ):
            for kind, cols in enumerate((slice(0, two), slice(two, width))):
                picked = rows[kind * slots : (kind + 1) * slots, :].astype(F32)
                picked = picked.reshape(-1, local_experts, CAPACITY, depth)[:, e]
                picked = picked.reshape(count, depth).astype(BF)
                totals[kind] += jnp.dot(picked, weights[e, :, cols], preferred_element_type=F32)
                if kind == 1:
                    grads[e] = picked
        terms_ref[here, :two] = totals[0].astype(BF)
        terms_ref[here, two:] = totals[1].astype(BF)


def activate(terms_ref, out_ref):
    copies, rows, width = out_ref.shape
    width = width // 3

    def total(part):
        cols = slice(part * width, (part + 1) * width)
        return sum(terms_ref[i, :, cols].astype(F32) for i in range(terms_ref.shape[0]))

    gate, up_proj, d_hidden = total(0), total(1), total(2)
    sigmoid_gate = jax.nn.sigmoid(gate)
    silu_gate = gate * sigmoid_gate
    hidden = (silu_gate * up_proj).astype(BF)
    d_gate = (d_hidden * up_proj * sigmoid_gate * (1.0 + gate * (1.0 - sigmoid_gate))).astype(BF)
    d_up = (d_hidden * silu_gate).astype(BF)
    for i in range(copies):
        out_ref[i, :, :width] = hidden
        out_ref[i, :, width : 2 * width] = d_gate
        out_ref[i, :, 2 * width :] = d_up


def last_terms(member_ref, acts_ref, kept_ref, other_ref, parts_ref):
    local_experts, depth, width = kept_ref.shape
    one = width // 3
    count = acts_ref.shape[0] // local_experts
    half = depth // 2
    for weights, member in ((kept_ref, member_ref[0]), (other_ref, 1 - member_ref[0])):
        outs, grads = [], []
        for e in range(local_experts):
            here = slice(e * count, (e + 1) * count)
            out = lax.dot_general(
                acts_ref[here, :one], weights[e, :, 2 * one :], NT, preferred_element_type=F32
            )
            grad = lax.dot_general(
                acts_ref[here, one:], weights[e, :, : 2 * one], NT, preferred_element_type=F32
            )
            outs.append(out.reshape(count // CAPACITY, CAPACITY, depth))
            grads.append(grad.reshape(count // CAPACITY, CAPACITY, depth))
        out, grad = jnp.concatenate(outs, axis=1), jnp.concatenate(grads, axis=1)
        for j in range(2):
            cols = slice(j * half, (j + 1) * half)
            parts_ref[2 * j + member, :, :, :half] = out[:, :, cols].astype(BF)
            parts_ref[2 * j + member, :, :, half:] = grad[:, :, cols].astype(BF)


def down_terms(acts_ref, grad_ref, other_grad_ref, out_ref, other_out_ref):
    local_experts, count, _ = grad_ref.shape
    one = out_ref.shape[1]
    for e in range(local_experts):
        hidden = acts_ref[e * count : (e + 1) * count, :one]
        for grads, out in ((grad_ref, out_ref), (other_grad_ref, other_out_ref)):
            out[e] = lax.dot_general(hidden, grads[e], TN, preferred_element_type=F32).astype(BF)


def add_parts(parts_ref, out_ref):
    out_ref[...] = sum(parts_ref[i].astype(F32) for i in range(parts_ref.shape[0])).astype(BF)


def combine(slot_ref, weights_ref, back_ref, mixed_ref, grads_ref):
    top_count, tok_rows = slot_ref.shape
    slots, width = back_ref.shape[0] // 2, back_ref.shape[1]
    half = width // 2
    same = iota((tok_rows, tok_rows), 0) == iota((tok_rows, tok_rows), 1)

    def column(row):
        return jnp.sum(jnp.where(same, row, 0.0), axis=1, keepdims=True)

    mixed = jnp.zeros((tok_rows, half), F32)
    grads = jnp.zeros((tok_rows, half), F32)
    for k in range(top_count):
        slot = column(slot_ref[k : k + 1, :].astype(F32)).astype(jnp.int32)
        hot = jnp.where(iota((tok_rows, slots), 1) == slot, 1.0, 0.0).astype(BF)
        picked = jnp.dot(hot, back_ref[:slots, :], preferred_element_type=F32) + jnp.dot(
            hot, back_ref[slots:, :], preferred_element_type=F32
        )
        mixed = mixed + picked[:, :half] * column(weights_ref[k : k + 1, :])
        grads = grads + picked[:, half:]
    mixed_ref[...] = mixed.astype(BF)
    grads_ref[...] = grads.astype(BF)


def exchange(rows, axis):
    return lax.all_to_all(rows, axis, split_axis=0, concat_axis=0, tiled=True)


def swap(block):
    return lax.ppermute(block, "ym", [(0, 1), (1, 0)])


def shards(tokens, routes, route_weights, gate_weight, up_weight, down_weight, cotangent):
    local_experts, depth, width = gate_weight.shape
    groups = lax.axis_size("z") * lax.axis_size("xl")
    experts = groups * local_experts
    tok_rows, top_count = routes.shape
    slots = experts * CAPACITY
    count = groups * CAPACITY
    half = width // 2
    slices = lax.axis_size("yp") * lax.axis_size("xh")
    core = lax.axis_index("exp").reshape(1)
    member = lax.axis_index("ym").reshape(1)
    routes, route_weights = routes.T, route_weights.T

    weights = shape((local_experts, depth, 3 * half), BF)
    send, slot_index, kept, given = call(
        functools.partial(begin, experts),
        (shape((slots, depth), BF), shape((top_count, tok_rows), jnp.int32), weights, weights),
        core, member, routes, route_weights, tokens, cotangent, gate_weight, up_weight,
        down_weight, scalars=2, given=7,
        scratch=[
            pltpu.VMEM(routes.shape, jnp.int32), pltpu.VMEM(routes.shape, F32),
            pltpu.VMEM(tokens.shape, BF), pltpu.VMEM(tokens.shape, BF),
            pltpu.VMEM(down_weight.shape, BF), pltpu.SemaphoreType.DMA((9,)),
        ],
    )
    other = swap(given)
    arrived = exchange(send, ETP)
    other_arrived = swap(arrived)
    rows = lax.all_gather(arrived, "exp", axis=0, tiled=True)
    other_rows = lax.all_gather(other_arrived, "exp", axis=0, tiled=True)

    grads = shape((local_experts, count, depth), BF)
    terms, expert_grad, other_grad = call(
        first_terms, (shape((slots, 3 * half), BF), grads, grads), kept, other, rows, other_rows
    )
    terms = exchange(terms, ("xh", "yp")).reshape(slices, slots // slices, 3 * half)
    acts = call(activate, shape(terms.shape, BF), terms)
    acts = exchange(acts.reshape(slots, 3 * half), ("xh", "yp"))

    parts = call(
        last_terms, shape((4, groups, local_experts * CAPACITY, depth), BF),
        member, acts, kept, other, scalars=1,
    )
    parts = exchange(parts.reshape(4 * slots, depth), "exp").reshape(2, 2 * slots, depth)
    slot_sums = call(add_parts, shape((2 * slots, depth), BF), parts)
    back = exchange(slot_sums, ("ym",) + ETP)
    downs = shape((local_experts, half, depth), BF)
    d_down, other_down = call(down_terms, (downs, downs), acts, expert_grad, other_grad)
    other_down = swap(other_down)
    first = member[0] == 0
    d_down = jnp.concatenate(
        [jnp.where(first, d_down, other_down), jnp.where(first, other_down, d_down)], axis=1
    )
    mixed, d_tokens = call(
        combine,
        (shape((tok_rows, depth // 2), BF), shape((tok_rows, depth // 2), BF)),
        slot_index, route_weights, back,
    )
    return mixed, d_tokens, d_down


def solution(mesh):
    fine = Mesh(mesh.devices.reshape(4, 2, 2, 2, 8, 4), ("yp", "ym", "xh", "exp", "z", "xl"))
    dp = ("yp", "ym", "xh")
    in_specs = (
        P(ETP, dp),
        P(ETP, None),
        P(ETP, None),
        P(ETP, dp, "exp"),
        P(ETP, dp, "exp"),
        P(ETP, "exp", dp),
        P(ETP, dp),
    )
    out_specs = (P(ETP, dp + ("exp",)), P(ETP, dp + ("exp",)), P(ETP, "exp", dp))
    return jax.shard_map(shards, mesh=fine, in_specs=in_specs, out_specs=out_specs, check_vma=False)
```
